128 devices in a mesh: seq: 4 (over y), ctx: 32 (over z, x, core).
Axes of the slice: x: 4, y: 4, z: 4, core: 2. Of those that a mesh axis runs over, the one named last changes fastest.
Arguments:
- tokens: bfloat16 [4, 4096, 768], P('seq', 'ctx'), may hold values from -6 to 6
- cotangent: bfloat16 [4, 4096, 768], P('seq', 'ctx'), may hold values from -6 to 6
- block_map: int32 [32, 2], replicated, may hold values from 0 to 63, as said below
- ln1_gain: bfloat16 [768], P(('seq', 'ctx')), may hold values from 0.5 to 1.5
- ln1_bias: bfloat16 [768], P(('seq', 'ctx')), may hold values from -1.5 to 1.5
- w_qkv: bfloat16 [768, 2304], P(('seq', 'ctx')), may hold values from -0.3125 to 0.3125
- b_query: bfloat16 [768], P(('seq', 'ctx')), may hold values from -2.5 to 2.5
- b_value: bfloat16 [768], P(('seq', 'ctx')), may hold values from -2.5 to 2.5
- w_out: bfloat16 [768, 768], P(('seq', 'ctx')), may hold values from -0.875 to 0.875
- b_out: bfloat16 [768], P(('seq', 'ctx')), may hold values from -1.5 to 1.5
- ln2_gain: bfloat16 [768], P(('seq', 'ctx')), may hold values from 0.5 to 1.5
- ln2_bias: bfloat16 [768], P(('seq', 'ctx')), may hold values from -1.5 to 1.5
- w_fc1: bfloat16 [768, 3072], P(('seq', 'ctx')), may hold values from -0.21875 to 0.21875
- b_fc1: bfloat16 [3072], P(('seq', 'ctx')), may hold values from -2.5 to 2.5
- w_fc2: bfloat16 [3072, 768], P(('seq', 'ctx')), may hold values from -0.109375 to 0.109375
- b_fc2: bfloat16 [768], P(('seq', 'ctx')), may hold values from -1.5 to 1.5
Outputs:
- mixed: bfloat16 [4, 4096, 768], P('seq', 'ctx')
- grad_tokens: bfloat16 [4, 4096, 768], P('seq', 'ctx')
- grad_ln1_gain: float32 [768], P(('seq', 'ctx'))
- grad_ln1_bias: float32 [768], P(('seq', 'ctx'))
- grad_w_qkv: float32 [768, 2304], P(('seq', 'ctx'))
- grad_b_query: float32 [768], P(('seq', 'ctx'))
- grad_b_value: float32 [768], P(('seq', 'ctx'))
- grad_w_out: float32 [768, 768], P(('seq', 'ctx'))
- grad_b_out: float32 [768], P(('seq', 'ctx'))
- grad_ln2_gain: float32 [768], P(('seq', 'ctx'))
- grad_ln2_bias: float32 [768], P(('seq', 'ctx'))
- grad_w_fc1: float32 [768, 3072], P(('seq', 'ctx'))
- grad_b_fc1: float32 [3072], P(('seq', 'ctx'))
- grad_w_fc2: float32 [3072, 768], P(('seq', 'ctx'))
- grad_b_fc2: float32 [768], P(('seq', 'ctx'))
The draws below stay inside these ranges and needn't reach their ends.
Inputs may be any that keep to these rules, and one draw needn't show every extreme that they name: `block_map`: row c names blocks p and 63 - p for some p; every p of 0 to 31 stands in exactly one row.
All inputs are finite; a program needn't handle non-finite values.
Results may differ from the reference program's by a relative error of at most 0.038.
Values may be sent and summed in bfloat16 or wider, within the bound.
No kernel may reach another device: no remote copies, remote signals or barrier semaphores. Data moves between devices by JAX's collectives and lax.ppermute only.
A program may use at most 128 MiB of HBM per device.

```python
from functools import partial
import jax
import jax.numpy as jnp
from jax import lax

D = 768
H = 12
HD = 64
FF = 3072
BLK = 64
BATCH = 4
SEQ_LEN = 4096
N_CTX = 32


def draw_block_map(key, part):
    key = jax.random.fold_in(key, 7)
    paired = jax.random.permutation(key, N_CTX).astype(jnp.int32)
    return jnp.stack([paired, 2 * N_CTX - 1 - paired], axis=1).astype(jnp.int32)


def strengthened(drawn, stream_key, source, target, parts, factor):
    owner, partner = [(jnp.arange(drawn.shape[dim]) // (drawn.shape[dim] // parts)).reshape([-1 if axis == dim else 1 for axis in range(drawn.ndim)]) for dim in (source, target)]
    chosen = jax.random.permutation(stream_key, parts)[partner]
    strong = (owner == chosen) | (owner == (partner + parts // 2) % parts)
    return jnp.where(strong, factor * drawn, drawn)


def levels(key, dims, split, low, high):
    def one(dim, shards_of):
        draws = jax.random.uniform(jax.random.fold_in(jax.random.fold_in(key, 6), dim), (shards_of,), jnp.float32, low / len(split), high / len(split))
        return jnp.repeat(jnp.exp(draws), dims[dim] // shards_of).reshape((-1,) + (1,) * (len(dims) - dim - 1))

    factor_of = one(*split[0])
    for cut in split[1:]:
        factor_of = factor_of * one(*cut)
    return factor_of


def scatter_about(own_key, shape, deviation, most, pieces=(), held_as=jnp.bfloat16):
    level = levels(own_key, shape, pieces, -0.22, 0.18) if pieces else 1.0
    drawn = jax.random.normal(own_key, shape, jnp.float32) * deviation * level
    return jnp.minimum(jnp.maximum(drawn, -most), most).astype(held_as)


def heavy_noise(rng, shape, scale, limit, pieces, heavy, kind=jnp.bfloat16):
    values = scale * jax.random.normal(rng, shape, jnp.float32)
    if pieces:
        values = values * levels(rng, shape, pieces, -0.22, 0.18)
    return jnp.clip(strengthened(values, jax.random.fold_in(rng, 3), *heavy), -limit, limit).astype(kind)


def setup_inputs(seed: int = 0) -> dict:
    keys = jax.random.split(jax.random.key(seed), 17)
    return {
        "tokens": scatter_about(keys[0], (BATCH, SEQ_LEN, D), 1.0, 6.0, ((0, 4), (1, 32))),
        "cotangent": heavy_noise(keys[1], (BATCH, SEQ_LEN, D), 1.0, 6.0, ((0, 4), (1, 32)), (1, 2, 32, 2.75)),
        "block_map": draw_block_map(jax.random.fold_in(keys[16], 71), 0),
        "ln1_gain": jnp.clip(1.0 + 0.1 * jax.random.normal(keys[3], (D,), jnp.float32), 0.5, 1.5).astype(jnp.bfloat16),
        "ln1_bias": scatter_about(keys[4], (D,), 0.3, 1.5, ((0, 128),)),
        "w_qkv": scatter_about(keys[5], (D, 3 * D), (D // 2) ** -0.5, 0.3125, ((0, 128),)),
        "b_query": scatter_about(keys[6], (D,), 0.5, 2.5, ((0, 128),)),
        "b_value": scatter_about(keys[7], (D,), 0.5, 2.5, ((0, 128),)),
        "w_out": scatter_about(keys[8], (D, D), (D // 16) ** -0.5, 0.875, ((0, 128),)),
        "b_out": scatter_about(keys[9], (D,), 0.3, 1.5, ((0, 128),)),
        "ln2_gain": jnp.clip(1.0 + 0.1 * jax.random.normal(keys[10], (D,), jnp.float32), 0.5, 1.5).astype(jnp.bfloat16),
        "ln2_bias": scatter_about(keys[11], (D,), 0.3, 1.5, ((0, 128),)),
        "w_fc1": scatter_about(keys[12], (D, FF), D ** -0.5, 0.21875, ((0, 128),)),
        "b_fc1": scatter_about(keys[13], (FF,), 0.5, 2.5, ((0, 128),)),
        "w_fc2": scatter_about(keys[14], (FF, D), FF ** -0.5, 0.109375, ((0, 128),)),
        "b_fc2": scatter_about(keys[15], (D,), 0.3, 1.5, ((0, 128),)),
    }


norm_eps = 1e-05
masked_fill = -1e+30

@jax.custom_vjp
def low(v):
    return lax.optimization_barrier(v.astype(jnp.bfloat16)).astype(jnp.float32)

@jax.custom_vjp
def low_back(v):
    return v

def low_keep(v):
    return (low(v), None)

def low_pass(kept, grad):
    return (grad,)

def back_keep(v):
    return (v, None)

def back_low(kept, grad):
    return (low(grad),)
low.defvjp(low_keep, low_pass)
low_back.defvjp(back_keep, back_low)

def layer_norm(values, gain, offset):
    row_mean = lax.optimization_barrier(jnp.mean(values, -1, keepdims=True))
    centered = values - row_mean
    variance = lax.optimization_barrier(jnp.mean(centered * centered, -1, keepdims=True))
    return centered * lax.rsqrt(variance + norm_eps) * gain + offset

def gelu_tanh(values):
    return jax.nn.gelu(values, approximate=True)

def positions(rows, block_span):
    rows = rows.reshape(-1).astype(jnp.int32)
    offsets = jnp.tile(jnp.arange(block_span, dtype=jnp.int32), rows.shape[0])
    return (jnp.repeat(rows, block_span) * block_span + offsets).astype(jnp.int32)

def attend(queries, key_rows, values, token_pos):
    total = queries.shape[0]
    span = min(512, total)
    score_scale = queries.shape[2] ** (-0.5)

    def one_block(start):
        query_block = lax.dynamic_slice_in_dim(queries, start, span, 0)
        query_pos = lax.dynamic_slice_in_dim(token_pos, start, span, 0)
        scores = jnp.einsum('qhd,khd->hqk', query_block, key_rows, precision=lax.Precision.HIGHEST) * score_scale
        scores = low_back(scores)
        allowed = (query_pos[:, None] >= token_pos[None, :])[None]
        scores = jnp.where(allowed, scores, masked_fill)
        row_top = lax.optimization_barrier(jnp.max(scores, -1, keepdims=True))
        expo = jnp.where(allowed, jnp.exp(scores - row_top), 0.0)
        probs = low(expo / lax.optimization_barrier(jnp.sum(expo, -1, keepdims=True)))
        return jnp.einsum('hqk,khd->qhd', probs, values, precision=lax.Precision.HIGHEST)
    block_starts = jnp.arange(total // span, dtype=jnp.int32) * span
    result = lax.map(jax.checkpoint(one_block), block_starts)
    return result.reshape(queries.shape)

def forward(token_rows, params, block_map):
    ln1_gain, ln1_bias, w_qkv, b_query, b_value, w_out, b_out, ln2_gain, ln2_bias, w_fc1, b_fc1, w_fc2, b_fc2 = params
    flat_rows = token_rows.reshape(-1, D)
    normed = low(layer_norm(flat_rows, ln1_gain, ln1_bias))
    qkv_bias = jnp.concatenate([b_query, jnp.zeros_like(b_query), b_value])
    qkv = jnp.dot(normed, w_qkv, precision=lax.Precision.HIGHEST) + qkv_bias
    qkv = low(low_back(qkv)).reshape(BATCH, SEQ_LEN, 3, H, HD)
    token_pos = positions(block_map, BLK)

    def per_sequence(triple):
        return attend(triple[0], triple[1], triple[2], token_pos)
    attended = lax.map(per_sequence, (qkv[:, :, 0], qkv[:, :, 1], qkv[:, :, 2]))
    attended = low(low_back(attended.reshape(-1, D)))
    branch = low_back(jnp.dot(attended, w_out, precision=lax.Precision.HIGHEST) + b_out)
    residual = flat_rows + branch
    normed_two = low(layer_norm(residual, ln2_gain, ln2_bias))
    hidden_pre = low_back(jnp.dot(normed_two, w_fc1, precision=lax.Precision.HIGHEST) + b_fc1)
    hidden_act = low(gelu_tanh(hidden_pre))
    result = residual + jnp.dot(hidden_act, w_fc2, precision=lax.Precision.HIGHEST) + b_fc2
    return result.reshape(token_rows.shape)

def reference(tokens, cotangent, block_map, ln1_gain, ln1_bias, w_qkv, b_query, b_value, w_out, b_out, ln2_gain, ln2_bias, w_fc1, b_fc1, w_fc2, b_fc2):
    params = tuple((p.astype(jnp.float32) for p in (ln1_gain, ln1_bias, w_qkv, b_query, b_value, w_out, b_out, ln2_gain, ln2_bias, w_fc1, b_fc1, w_fc2, b_fc2)))
    token_rows = tokens.astype(jnp.float32)
    result, pullback = jax.vjp(partial(forward, block_map=block_map), token_rows, params)
    grad_rows, grads = pullback(cotangent.astype(jnp.float32))
    return (result.astype(jnp.bfloat16), grad_rows.astype(jnp.bfloat16), grads[0], grads[1], grads[2], grads[3], grads[4], grads[5], grads[6], grads[7], grads[8], grads[9], grads[10], grads[11], grads[12])
```

```python
import jax
import jax.numpy as jnp
import numpy as np
from jax import lax
from jax.experimental import pallas as pl
from jax.experimental.pallas import tpu as pltpu
from jax.sharding import Mesh, PartitionSpec as P

D = 768
H = 12
HD = 64
FF = 3072
BLK = 64
TP = 4
HL = H // TP
HW = HL * HD
TOK = 128
ROWS = TOK * TP
KEYS = 4096
CHUNK = 512
EPS = 1e-05
MASKED = -1e30
LOG2E = 1.4426950408889634
SCALE = HD**-0.5
BF = jnp.bfloat16
F32 = jnp.float32
G = ("c", "y", "z")


def natural_feature(i):
    c, y, z, x, r = i // 384, (i // 96) % 4, (i // 24) % 4, (i // 6) % 4, i % 6
    return y * 192 + z * 48 + x * 12 + c * 6 + r


def feature_matrix():
    out = np.zeros((D, D), np.float32)
    i = np.arange(D)
    out[natural_feature(i), i] = 1
    return out.astype(jnp.bfloat16)


def head_matrix():
    out = np.zeros((3 * HW, 6 * 2 * HD), np.float32)
    for h in range(HL):
        for d in range(HD):
            out[HW + h * HD + d, h * 128 + d] = 1
            out[2 * HW + h * HD + d, h * 128 + HD + d] = 1
            out[h * HD + d, 384 + h * 128 + d] = 1
    return out.astype(jnp.bfloat16)


def dot(a, b):
    return lax.dot_general(a, b, (((1,), (0,)), ((), ())), preferred_element_type=F32)


def dot_nt(a, b):
    return lax.dot_general(a, b, (((1,), (1,)), ((), ())), preferred_element_type=F32)


def dot_tn(a, b):
    return lax.dot_general(a, b, (((0,), (0,)), ((), ())), preferred_element_type=F32)


def standardized(v):
    mean = jnp.mean(v, -1, keepdims=True)
    centered = v - mean
    rstd = lax.rsqrt(jnp.mean(centered * centered, -1, keepdims=True) + EPS)
    return centered * rstd, rstd


def norm_back(g, xhat, rstd):
    return rstd * (
        g - jnp.mean(g, -1, keepdims=True) - xhat * jnp.mean(g * xhat, -1, keepdims=True)
    )


def gelu_pair(u):
    k = 0.7978845608028654
    t = jnp.tanh(k * (u + 0.044715 * u * u * u))
    value = 0.5 * u * (1 + t)
    slope = 0.5 * (1 + t) + 0.5 * u * (1 - t * t) * k * (1 + 3 * 0.044715 * u * u)
    return value, slope


TILES = ((0, KEYS // 2), (ROWS // 2, KEYS))


def scores_t(kv, q, qpos, start, masked):
    s = dot_nt(kv, q)
    if masked:
        key = lax.broadcasted_iota(jnp.int32, s.shape, 0) + start
        s = jnp.where(key <= qpos, s, MASKED)
    return s


def attend_kernel(kpos, rank, qpos_ref, q_ref, kv_ref, o_ref, lse_ref, kvs_ref, kvt_ref, qs_ref):
    for b in range(KEYS // BLK):
        at = pl.multiple_of(kpos[b] * BLK, BLK)
        kvs_ref[pl.ds(at, BLK), :] = kv_ref[b * BLK : (b + 1) * BLK, :]
    for b in range(ROWS // BLK):
        at = pl.multiple_of(rank[b] * BLK, BLK)
        qs_ref[pl.ds(at, BLK), :] = q_ref[b * BLK : (b + 1) * BLK, :] * SCALE
    for i in range(KEYS // CHUNK):
        kvt_ref[:, i * CHUNK : (i + 1) * CHUNK] = kvs_ref[i * CHUNK : (i + 1) * CHUNK, :].T
    for first, span in TILES:
        q = qs_ref[first : first + 256, :]
        qpos = qpos_ref[0:1, first : first + 256]
        top = jnp.full((1, 256), MASKED, F32)
        mass = jnp.zeros((1, 256), F32)
        acc = jnp.zeros((128, 256), F32)
        for start in range(0, span, CHUNK):
            s = scores_t(
                kvs_ref[start : start + CHUNK, :], q, qpos, start, start + CHUNK > span - KEYS // 2
            )
            new = jnp.maximum(top, jnp.max(s, 0, keepdims=True))
            p = jnp.exp2((s - new) * LOG2E)
            alpha = jnp.exp2((top - new) * LOG2E)
            mass = mass * alpha + jnp.sum(p, 0, keepdims=True)
            acc = acc * alpha + dot(kvt_ref[:, start : start + CHUNK], p.astype(BF))
            top = new
        o_ref[:, first : first + 256] = acc[HD:, :] * (1.0 / mass)
        lse_ref[0, :, first : first + 256] = jnp.broadcast_to(
            top * LOG2E + jnp.log2(mass), (8, 256)
        )


def attend_back_kernel(
    kpos, rank, qpos_ref, qs_ref, kvs_ref, kvt_ref, do_ref, o_ref, lse_ref, dkv_ref, dq_ref, dos, acc
):
    for b in range(ROWS // BLK):
        at = pl.multiple_of(rank[b] * BLK, BLK)
        dos[pl.ds(at, BLK), :] = do_ref[b * BLK : (b + 1) * BLK, :]
    dot_t = dos[...].astype(F32).T
    delta = jnp.sum(dot_t[HD:, :] * o_ref[...], 0, keepdims=True)
    dq = [jnp.zeros((128, 256), F32), jnp.zeros((128, 256), F32)]
    for start in range(0, KEYS, CHUNK):
        kv = kvs_ref[start : start + CHUNK, :]
        kvt = kvt_ref[:, start : start + CHUNK]
        total = None
        for n, (first, span) in enumerate(TILES):
            if start >= span:
                continue
            cols = slice(first, first + 256)
            q = qs_ref[cols, :]
            do = dos[cols, :]
            s = scores_t(kv, q, qpos_ref[0:1, cols], start, start + CHUNK > span - KEYS // 2)
            p = jnp.exp2(s * LOG2E - lse_ref[0, 0:1, cols])
            dp = dot_nt(kv, do)
            ds = (p * (dp - delta[:, cols])).astype(BF)
            part = dot(ds, q) + dot(p.astype(BF), do)
            total = part if total is None else total + part
            dq[n] = dq[n] + dot(kvt, ds)
        acc[start : start + CHUNK, :] = total.astype(BF)
    for b in range(KEYS // BLK):
        at = pl.multiple_of(kpos[b] * BLK, BLK)
        dkv_ref[b * BLK : (b + 1) * BLK, :] = acc[pl.ds(at, BLK), :]
    dos[0:256, :] = (dq[0] * SCALE).T.astype(BF)
    dos[256:512, :] = (dq[1] * SCALE).T.astype(BF)
    for b in range(ROWS // BLK):
        at = pl.multiple_of(rank[b] * BLK, BLK)
        dq_ref[b * BLK : (b + 1) * BLK, :] = dos[pl.ds(at, BLK), :]


PARAMS = dict(compiler_params=pltpu.CompilerParams(vmem_limit_bytes=48 * 1024 * 1024))


def attend(kpos, rank, qpos, q, kv):
    grid_spec = pltpu.PrefetchScalarGridSpec(
        num_scalar_prefetch=2,
        grid=(HL,),
        in_specs=[
            pl.BlockSpec((8, ROWS), lambda h, *_: (0, 0)),
            pl.BlockSpec((ROWS, 128), lambda h, *_: (0, h)),
            pl.BlockSpec((KEYS, 128), lambda h, *_: (0, h)),
        ],
        out_specs=[
            pl.BlockSpec((HD, ROWS), lambda h, *_: (h, 0)),
            pl.BlockSpec((1, 8, ROWS), lambda h, *_: (h, 0, 0)),
            pl.BlockSpec((KEYS, 128), lambda h, *_: (0, h)),
            pl.BlockSpec((128, KEYS), lambda h, *_: (h, 0)),
            pl.BlockSpec((ROWS, 128), lambda h, *_: (0, h)),
        ],
    )
    return pl.pallas_call(
        attend_kernel,
        grid_spec=grid_spec,
        out_shape=[
            jax.ShapeDtypeStruct((HW, ROWS), F32),
            jax.ShapeDtypeStruct((HL, 8, ROWS), F32),
            jax.ShapeDtypeStruct((KEYS, 384), BF),
            jax.ShapeDtypeStruct((384, KEYS), BF),
            jax.ShapeDtypeStruct((ROWS, 384), BF),
        ],
        name="attend",
        **PARAMS,
    )(kpos, rank, qpos, q, kv)


def attend_back(kpos, rank, qpos, qs, kvs, kvt, do, o, lse):
    grid_spec = pltpu.PrefetchScalarGridSpec(
        num_scalar_prefetch=2,
        grid=(HL,),
        in_specs=[
            pl.BlockSpec((8, ROWS), lambda h, *_: (0, 0)),
            pl.BlockSpec((ROWS, 128), lambda h, *_: (0, h)),
            pl.BlockSpec((KEYS, 128), lambda h, *_: (0, h)),
            pl.BlockSpec((128, KEYS), lambda h, *_: (h, 0)),
            pl.BlockSpec((ROWS, 128), lambda h, *_: (0, h)),
            pl.BlockSpec((HD, ROWS), lambda h, *_: (h, 0)),
            pl.BlockSpec((1, 8, ROWS), lambda h, *_: (h, 0, 0)),
        ],
        out_specs=[
            pl.BlockSpec((KEYS, 128), lambda h, *_: (0, h)),
            pl.BlockSpec((ROWS, 128), lambda h, *_: (0, h)),
        ],
        scratch_shapes=[pltpu.VMEM((ROWS, 128), BF), pltpu.VMEM((KEYS, 128), BF)],
    )
    return pl.pallas_call(
        attend_back_kernel,
        grid_spec=grid_spec,
        out_shape=[
            jax.ShapeDtypeStruct((KEYS, 384), BF),
            jax.ShapeDtypeStruct((ROWS, 384), BF),
        ],
        name="attend_back",
        **PARAMS,
    )(kpos, rank, qpos, qs, kvs, kvt, do, o, lse)


def exchange(v, axes):
    return lax.all_to_all(v, axes, 0, 0, tiled=True)


def spread(v, axes, n):
    return exchange(jnp.broadcast_to(v[None], (n,) + v.shape), axes)


def per_device(
    tokens,
    cotangent,
    block_map,
    ln1_gain,
    ln1_bias,
    w_qkv,
    b_query,
    b_value,
    w_out,
    b_out,
    ln2_gain,
    ln2_bias,
    w_fc1,
    b_fc1,
    w_fc2,
    b_fc2,
):
    perm = jnp.asarray(feature_matrix())
    heads = jnp.asarray(head_matrix())
    z, x, c = lax.axis_index("z"), lax.axis_index("x"), lax.axis_index("c")
    perm_t = lax.dynamic_slice_in_dim(perm, x * HW, HW, 0)

    maps = block_map.reshape(4, 4, 2, 2).transpose(2, 0, 1, 3)
    kpos = maps.reshape(-1)
    own = lax.dynamic_slice(maps, (c, z, 0, 0), (1, 1, 4, 2)).reshape(-1)
    before = own[None, :] < own[:, None]
    rank = jnp.sum(before.astype(jnp.int32), 1)
    ordered = jnp.sum(jnp.where(rank[:, None] == jnp.arange(8)[None, :], own[:, None], 0), 0)
    qpos = (ordered[:, None] * BLK + jnp.arange(BLK, dtype=jnp.int32)[None, :]).reshape(1, -1)
    qpos = jnp.broadcast_to(qpos, (8, ROWS))

    own_rows = dot(jnp.concatenate([tokens[0], cotangent[0]], 0), perm).astype(BF)
    all_rows = lax.all_gather(own_rows, "x", axis=0)
    tok = all_rows[:, :TOK].reshape(ROWS, D)
    dy = all_rows[:, TOK:].reshape(ROWS, D)
    own_tok = own_rows[:TOK].astype(F32)
    own_dy = own_rows[TOK:].astype(F32)

    out_cols = dot(jnp.concatenate([w_out, w_fc2], 0), perm).astype(BF)
    vectors = jnp.stack([ln1_gain, ln1_bias, b_query, b_value, b_out, ln2_gain, ln2_bias, b_fc2], 1)
    vectors = jnp.pad(vectors, ((0, 0), (0, 120)))
    qkv_cols = w_qkv.reshape(6, 3, TP, HW).transpose(2, 0, 1, 3).reshape(TP, 6, 3 * HW)
    fc1_cols = w_fc1.reshape(6, 16, TP, 2, 24).transpose(2, 0, 3, 1, 4).reshape(TP, 6, D)
    everyone = jnp.concatenate([vectors, out_cols[:6]], 1)
    sent = jnp.concatenate(
        [qkv_cols, fc1_cols, jnp.broadcast_to(everyone[None], (TP,) + everyone.shape)], 2
    )
    got = exchange(sent, "x").reshape(24, -1)
    extras = jnp.where(
        jnp.arange(128)[None, :] == 8, b_fc1[:, None], got[:, 1344:1472]
    )
    first = spread(jnp.concatenate([got[:, :576], extras], 1), G, 32).reshape(D, 704)
    second = lax.all_gather(
        jnp.concatenate([got[:, 576:1344], got[:, 1472:], out_cols[6:]], 1), G, axis=0, tiled=True
    )
    vec = first[:, 576:592].astype(F32).T
    gain1, bias1, bout, gain2, bias2, bfc2, bfc1 = (
        vec[i : i + 1] for i in (0, 1, 4, 5, 6, 7, 8)
    )
    bqv = dot_nt(first[:, 578:580].T, perm_t)
    bias_t = jnp.concatenate([bqv[0:1], jnp.zeros((1, HW), F32), bqv[1:2]], 1)
    bias_pad = dot(bias_t.astype(BF), heads)
    w_heads = dot(first[:, :576], heads).astype(BF)

    hat1, _ = standardized(tok.astype(F32))
    a1 = (hat1 * gain1 + bias1).astype(BF)
    qkv = (dot(a1, w_heads) + bias_pad).astype(BF)
    kv = spread(qkv[:, :384], "z", 4).reshape(4 * ROWS, 384)
    kv = lax.all_gather(kv, "c", axis=0, tiled=True)
    o_t, lse, kvs, kvt, qs = attend(kpos, rank, qpos, qkv[:, 384:], kv)

    place = jnp.repeat(rank, BLK) * BLK + jnp.tile(jnp.arange(BLK, dtype=jnp.int32), 8)
    unsort = (place[:, None] == jnp.arange(ROWS, dtype=jnp.int32)[None, :]).astype(BF)
    o = dot_nt(unsort, o_t.astype(BF)).astype(BF)
    o_all = spread(o, "x", 4)
    o_perm = sum(dot(o_all[i], perm[i * HW : (i + 1) * HW]) for i in range(TP)).astype(BF)

    w1, wo, w2 = second[:, :D], second[:, D : 2 * D], second[:, 2 * D :]
    resid = tok.astype(F32) + dot(o_perm, wo) + bout
    hat2, _ = standardized(resid)
    a2 = (hat2 * gain2 + bias2).astype(BF)
    u = dot(a2, w1) + bfc1
    act, slope = gelu_pair(u)
    gb = act.astype(BF)
    du = (dot_nt(dy, w2) * slope).astype(BF)
    mixed_part = dot(gb, w2).astype(BF)
    da2_part = dot_nt(du, w1).astype(BF)
    g_fc2 = dot_tn(gb, dy).astype(BF)
    g_fc1 = dot_tn(a2, du).astype(BF)
    g_bfc1 = jnp.sum(du.astype(F32), 0)

    parts = jnp.concatenate(
        [mixed_part.reshape(TP, TOK, D), da2_part.reshape(TP, TOK, D)], 1
    )
    sums = jnp.sum(exchange(parts, "x").astype(F32), 0)
    own_resid = lax.dynamic_slice_in_dim(resid, x * TOK, TOK, 0)
    mixed = (own_resid + sums[:TOK] + bfc2).astype(BF)
    da2 = sums[TOK:]
    hat2o, rstd2 = standardized(own_resid)
    g_gain2 = jnp.sum(da2 * hat2o, 0)
    g_bias2 = jnp.sum(da2, 0)
    dresid = own_dy + norm_back(da2 * gain2, hat2o, rstd2)
    dbranch = dresid.astype(BF)
    g_bout = jnp.sum(dbranch.astype(F32), 0)
    g_bfc2 = jnp.sum(own_dy, 0)
    dbr = spread(dbranch, "x", 4).reshape(ROWS, D)

    wo_t = dot(perm_t, wo).astype(BF)
    wo_pad = dot_tn(heads[2 * HW :, :384], wo_t).astype(BF)
    do = dot_nt(dbr, wo_pad).astype(BF)
    dkv_part, dq = attend_back(kpos, rank, qpos, qs, kvs, kvt, do, o_t, lse)
    dkv_c = exchange(dkv_part, "c").reshape(2, KEYS // 2, 384)
    dkv_c = (dkv_c[0].astype(F32) + dkv_c[1].astype(F32)).astype(BF)
    dkv_z = exchange(dkv_c, "z").reshape(4, ROWS, 384)
    dkv = jnp.sum(dkv_z.astype(F32), 0).astype(BF)
    dqkv = dot_nt(jnp.concatenate([dkv, dq], 1), heads).astype(BF)
    da1_part = dot_nt(dqkv, first[:, :576])
    g_gain1 = jnp.sum(da1_part * hat1, 0)
    g_bias1 = jnp.sum(da1_part, 0)
    g_qkv = dot_tn(a1, dqkv).astype(BF)
    dqkv_sum = jnp.sum(dqkv.astype(F32), 0)
    g_bqv = dot(jnp.stack([dqkv_sum[:HW], dqkv_sum[2 * HW :]], 0).astype(BF), perm_t)
    dbr_t = lax.dynamic_slice_in_dim(dbr, x * HW, HW, 1)
    g_out = dot_tn(o_perm, dbr_t).astype(BF)

    da1 = jnp.sum(exchange(da1_part.astype(BF).reshape(TP, TOK, D), "x").astype(F32), 0)
    hat1o, rstd1 = standardized(own_tok)
    dtok = (dresid + norm_back(da1 * gain1, hat1o, rstd1)).astype(BF)
    back = dot_nt(jnp.concatenate([mixed, dtok], 0), perm).astype(BF)
    mixed, dtok = back[:TOK], back[TOK:]

    rows = jnp.stack(
        [g_gain1, g_bias1, g_bqv[0], g_bqv[1], g_bout, g_gain2, g_bias2, g_bfc2, g_bfc1], 0
    )
    columns = jnp.pad(rows, ((0, 119), (0, 0))).T.astype(BF)
    grads = jnp.concatenate([g_qkv, g_fc1, g_out, columns, g_fc2], 1)
    half = exchange(grads, "c").reshape(2, D // 2, -1)
    half = (half[0].astype(F32) + half[1].astype(F32)).astype(BF)
    mine = jnp.sum(exchange(half, ("y", "z")).reshape(16, 24, -1).astype(F32), 0)
    last = exchange(mine[:, :1664].reshape(TP, 6, 1664), "x")
    r_qkv = last[:, :, :576].reshape(TP, 6, 3, HW).transpose(1, 2, 0, 3).reshape(6, 3 * D)
    r_fc1 = (
        last[:, :, 576:1344].reshape(TP, 6, 2, 16, 24).transpose(1, 3, 0, 2, 4).reshape(6, FF)
    )
    r_out = last[:, :, 1344:1536].transpose(1, 0, 2).reshape(6, D)
    r_vec = jnp.sum(last[:, :, 1536:1544], 0)
    r_cols = lax.dot_general(
        jnp.concatenate([r_out, mine[:, 1664:]], 0),
        perm.astype(F32),
        (((1,), (1,)), ((), ())),
        precision=lax.Precision.HIGHEST,
    )
    return (
        mixed[None],
        dtok[None],
        r_vec[:, 0],
        r_vec[:, 1],
        r_qkv,
        r_vec[:, 2],
        r_vec[:, 3],
        r_cols[:6],
        r_vec[:, 4],
        r_vec[:, 5],
        r_vec[:, 6],
        r_fc1,
        mine[:, 1544],
        r_cols[6:],
        r_vec[:, 7],
    )


def solution(mesh):
    fine = Mesh(mesh.devices.reshape(4, 4, 4, 2), ("y", "z", "x", "c"))
    rows = P("y", ("z", "x", "c"), None)
    every = ("y", "z", "x", "c")
    vec, mat = P(every), P(every, None)
    in_specs = (rows, rows, P(), vec, vec, mat, vec, vec, mat, vec, vec, vec, mat, vec, mat, vec)
    out_specs = (rows, rows, vec, vec, mat, vec, vec, mat, vec, vec, vec, mat, vec, mat, vec)
    return jax.shard_map(
        per_device, mesh=fine, in_specs=in_specs, out_specs=out_specs, check_vma=False
    )
```

```python
import jax
import jax.numpy as jnp
import numpy as np
from jax import lax
from jax.experimental import pallas as pl
from jax.experimental.pallas import tpu as pltpu
from jax.sharding import Mesh, PartitionSpec as P

D = 768
H = 12
HD = 64
FF = 3072
BLK = 64
TP = 4
HL = H // TP
HW = HL * HD
COLS = 640
TOK = 128
ROWS = TOK * TP
KEYS = 4096
CHUNK = 1024
BACK = 2048
EPS = 1e-05
MASKED = -1e30
LOG2E = 1.4426950408889634
SCALE = HD**-0.5
BF = jnp.bfloat16
F32 = jnp.float32
G = ("c", "y", "z")
SWAP = ((0, 1), (1, 0))


def natural_feature(i):
    c, y, z, x, r = i // 384, (i // 96) % 4, (i // 24) % 4, (i // 6) % 4, i % 6
    return y * 192 + z * 48 + x * 12 + c * 6 + r


def feature_matrix():
    out = np.zeros((D, D), np.float32)
    i = np.arange(D)
    out[natural_feature(i), i] = 1
    return out.astype(jnp.bfloat16)


def head_matrix():
    out = np.zeros((COLS, 6 * 2 * HD), np.float32)
    for h in range(HL):
        for d in range(HD):
            out[HW + h * HD + d, h * 128 + d] = 1
            out[2 * HW + h * HD + d, h * 128 + HD + d] = 1
            out[h * HD + d, 384 + h * 128 + d] = 1
    return out.astype(jnp.bfloat16)


def dot(a, b):
    return lax.dot_general(a, b, (((1,), (0,)), ((), ())), preferred_element_type=F32)


def dot_nt(a, b):
    return lax.dot_general(a, b, (((1,), (1,)), ((), ())), preferred_element_type=F32)


def dot_tn(a, b):
    return lax.dot_general(a, b, (((0,), (0,)), ((), ())), preferred_element_type=F32)


def standardized(v):
    mean = jnp.mean(v, -1, keepdims=True)
    centered = v - mean
    rstd = lax.rsqrt(jnp.mean(centered * centered, -1, keepdims=True) + EPS)
    return centered * rstd, rstd


def norm_back(g, xhat, rstd):
    return rstd * (
        g - jnp.mean(g, -1, keepdims=True) - xhat * jnp.mean(g * xhat, -1, keepdims=True)
    )


def gelu_pair(u):
    k = 0.7978845608028654
    t = jnp.tanh(k * (u + 0.044715 * u * u * u))
    value = 0.5 * u * (1 + t)
    slope = 0.5 * (1 + t) + 0.5 * u * (1 - t * t) * k * (1 + 3 * 0.044715 * u * u)
    return value, slope


TILES = ((0, KEYS // 2), (ROWS // 2, KEYS))


def scores_t(kv, q, qpos, start, masked):
    s = dot_nt(kv, q)
    if masked:
        key = lax.broadcasted_iota(jnp.int32, s.shape, 0) + start
        s = jnp.where(key <= qpos, s, MASKED)
    return s


def attend_kernel(
    kpos, rank, qpos_ref, q_ref, own_ref, other_ref, o_ref, ot_ref, lse_ref, kvs_ref, kvt_ref, qs_ref, o_s, o_r
):
    head = pl.program_id(0)
    for b in range(KEYS // BLK):
        at = pl.multiple_of(kpos[b] * BLK, BLK)
        part = own_ref if b < KEYS // BLK // 2 else other_ref
        row = b % (KEYS // BLK // 2) * BLK
        kvs_ref[pl.ds(at, BLK), :] = part[row : row + BLK, :]
    for b in range(ROWS // BLK):
        at = pl.multiple_of(rank[b] * BLK, BLK)
        qs_ref[pl.ds(at, BLK), :] = q_ref[b * BLK : (b + 1) * BLK, :] * SCALE
    for i in range(KEYS // CHUNK):
        kvt_ref[:, i * CHUNK : (i + 1) * CHUNK] = kvs_ref[i * CHUNK : (i + 1) * CHUNK, :].T
    for first, span in TILES:
        q = qs_ref[first : first + 256, :]
        qpos = qpos_ref[0:1, first : first + 256]
        top = jnp.full((8, 256), MASKED, F32)
        for start in range(0, span, CHUNK):
            masked = start + CHUNK > span - KEYS // 2
            s = scores_t(kvs_ref[start : start + CHUNK, :], q, qpos, start, masked)
            top = jnp.maximum(top, jnp.max(s.reshape(-1, 8, 256), 0))
        top = jnp.max(top, 0, keepdims=True) * LOG2E
        mass = jnp.zeros((8, 256), F32)
        acc = jnp.zeros((128, 256), F32)
        for start in range(0, span, CHUNK):
            masked = start + CHUNK > span - KEYS // 2
            s = scores_t(kvs_ref[start : start + CHUNK, :], q, qpos, start, masked)
            p = jnp.exp2(s * LOG2E - top)
            mass = mass + jnp.sum(p.reshape(-1, 8, 256), 0)
            acc = acc + dot(kvt_ref[:, start : start + CHUNK], p.astype(BF))
        mass = jnp.sum(mass, 0, keepdims=True)
        o = acc[HD:, :] * (1.0 / mass)
        ot_ref[:, first : first + 256] = o
        o_s[pl.ds(pl.multiple_of(head * HD, HD), HD), first : first + 256] = o
        lse_ref[0, :, first : first + 256] = jnp.broadcast_to(top + jnp.log2(mass), (8, 256))

    @pl.when(head == HL - 1)
    def _():
        o_r[...] = o_s[...].T.astype(BF)
        for b in range(ROWS // BLK):
            at = pl.multiple_of(rank[b] * BLK, BLK)
            row, col = b * BLK % TOK, b * BLK // TOK * HW
            o_ref[row : row + BLK, col : col + HW] = o_r[pl.ds(at, BLK), :]


def attend_back_kernel(
    kpos,
    rank,
    qpos_ref,
    qs_ref,
    kvs_ref,
    kvt_ref,
    dbr_ref,
    wo_ref,
    o_ref,
    lse_ref,
    own_ref,
    other_ref,
    dq_ref,
    dos,
    acc,
):
    do_all = dot_nt(dbr_ref[...], wo_ref[...]).astype(BF)
    for b in range(ROWS // BLK):
        at = pl.multiple_of(rank[b] * BLK, BLK)
        dos[pl.ds(at, BLK), :] = do_all[b * BLK : (b + 1) * BLK, :]
    dot_t = dos[...].astype(F32).T
    delta = jnp.sum(dot_t[HD:, :] * o_ref[...], 0, keepdims=True)
    dq = [jnp.zeros((128, 256), F32), jnp.zeros((128, 256), F32)]
    for start in range(0, KEYS, BACK):
        kv = kvs_ref[start : start + BACK, :]
        kvt = kvt_ref[:, start : start + BACK]
        total = None
        for n, (first, span) in enumerate(TILES):
            if start >= span:
                continue
            cols = slice(first, first + 256)
            q = qs_ref[cols, :]
            do = dos[cols, :]
            s = scores_t(kv, q, qpos_ref[0:1, cols], start, start + BACK > span - KEYS // 2)
            p = jnp.exp2(s * LOG2E - lse_ref[0, 0:1, cols])
            dp = dot_nt(kv, do)
            ds = (p * (dp - delta[:, cols])).astype(BF)
            part = dot(ds, q) + dot(p.astype(BF), do)
            total = part if total is None else total + part
            dq[n] = dq[n] + dot(kvt, ds)
        acc[start : start + BACK, :] = total.astype(BF)
    for b in range(KEYS // BLK):
        at = pl.multiple_of(kpos[b] * BLK, BLK)
        part = own_ref if b < KEYS // BLK // 2 else other_ref
        row = b % (KEYS // BLK // 2) * BLK
        part[row : row + BLK, :] = acc[pl.ds(at, BLK), :]
    dos[0:256, :] = (dq[0] * SCALE).T.astype(BF)
    dos[256:512, :] = (dq[1] * SCALE).T.astype(BF)
    for b in range(ROWS // BLK):
        at = pl.multiple_of(rank[b] * BLK, BLK)
        dq_ref[b * BLK : (b + 1) * BLK, :] = dos[pl.ds(at, BLK), :]


def settings(flops):
    return dict(
        compiler_params=pltpu.CompilerParams(vmem_limit_bytes=56 * 1024 * 1024),
        cost_estimate=pl.CostEstimate(flops=flops, bytes_accessed=8_000_000, transcendentals=0),
    )


def shape(dims, kind=BF):
    return jax.ShapeDtypeStruct(dims, kind)


def attend(kpos, rank, qpos, q, own, other):
    grid_spec = pltpu.PrefetchScalarGridSpec(
        num_scalar_prefetch=2,
        grid=(HL,),
        in_specs=[
            pl.BlockSpec((8, ROWS), lambda h, *_: (0, 0)),
            pl.BlockSpec((ROWS, 128), lambda h, *_: (0, h)),
            pl.BlockSpec((KEYS // 2, 128), lambda h, *_: (0, h)),
            pl.BlockSpec((KEYS // 2, 128), lambda h, *_: (0, h)),
        ],
        out_specs=[
            pl.BlockSpec((TOK, D), lambda h, *_: (0, 0)),
            pl.BlockSpec((HD, ROWS), lambda h, *_: (h, 0)),
            pl.BlockSpec((1, 8, ROWS), lambda h, *_: (h, 0, 0)),
            pl.BlockSpec((KEYS, 128), lambda h, *_: (0, h)),
            pl.BlockSpec((128, KEYS), lambda h, *_: (h, 0)),
            pl.BlockSpec((ROWS, 128), lambda h, *_: (0, h)),
        ],
        scratch_shapes=[pltpu.VMEM((HW, ROWS), F32), pltpu.VMEM((ROWS, HW), BF)],
    )
    return pl.pallas_call(
        attend_kernel,
        grid_spec=grid_spec,
        out_shape=[
            shape((TOK, D)),
            shape((HW, ROWS), F32),
            shape((HL, 8, ROWS), F32),
            shape((KEYS, 384)),
            shape((384, KEYS)),
            shape((ROWS, 384)),
        ],
        name="attend",
        **settings(5_000_000_000),
    )(kpos, rank, qpos, q, own, other)


def attend_back(kpos, rank, qpos, qs, kvs, kvt, dbr, wo, o, lse):
    grid_spec = pltpu.PrefetchScalarGridSpec(
        num_scalar_prefetch=2,
        grid=(HL,),
        in_specs=[
            pl.BlockSpec((8, ROWS), lambda h, *_: (0, 0)),
            pl.BlockSpec((ROWS, 128), lambda h, *_: (0, h)),
            pl.BlockSpec((KEYS, 128), lambda h, *_: (0, h)),
            pl.BlockSpec((128, KEYS), lambda h, *_: (h, 0)),
            pl.BlockSpec((ROWS, D), lambda h, *_: (0, 0)),
            pl.BlockSpec((128, D), lambda h, *_: (h, 0)),
            pl.BlockSpec((HD, ROWS), lambda h, *_: (h, 0)),
            pl.BlockSpec((1, 8, ROWS), lambda h, *_: (h, 0, 0)),
        ],
        out_specs=[
            pl.BlockSpec((KEYS // 2, 128), lambda h, *_: (0, h)),
            pl.BlockSpec((KEYS // 2, 128), lambda h, *_: (0, h)),
            pl.BlockSpec((ROWS, 128), lambda h, *_: (0, h)),
        ],
        scratch_shapes=[pltpu.VMEM((ROWS, 128), BF), pltpu.VMEM((KEYS, 128), BF)],
    )
    return pl.pallas_call(
        attend_back_kernel,
        grid_spec=grid_spec,
        out_shape=[shape((KEYS // 2, 384)), shape((KEYS // 2, 384)), shape((ROWS, 384))],
        name="attend_back",
        **settings(15_000_000_000),
    )(kpos, rank, qpos, qs, kvs, kvt, dbr, wo, o, lse)


GAIN1, BIAS1, BQ, BV, BOUT, GAIN2, BIAS2, BFC2, BFC1 = range(9)


def project_kernel(
    c_ref, rows_ref, own_ref, other_ref, heads_ref, perm_t_ref, a1_ref, kv_ref, q_ref, vec_ref, w_ref
):
    c = c_ref[0]
    w_ref[pl.ds(pl.multiple_of(c * (D // 2), D // 2), D // 2), :] = own_ref[...]
    w_ref[pl.ds(pl.multiple_of((1 - c) * (D // 2), D // 2), D // 2), :] = other_ref[...]
    vec = w_ref[:, 512:].astype(F32).T[64:80]
    vec_ref[...] = vec
    bqv = dot_nt(vec[0:8].astype(BF), perm_t_ref[...]).astype(BF)
    bias = (
        dot(bqv, heads_ref[0:HW, :])[BQ : BQ + 1]
        + dot(bqv, heads_ref[2 * HW : 3 * HW, :])[BV : BV + 1]
    )
    w = dot(w_ref[...], heads_ref[...]).astype(BF)
    for i in range(TP):
        at = slice(i * TOK, (i + 1) * TOK)
        hat, _ = standardized(rows_ref[i, 0:TOK, :].astype(F32))
        a1_ref[at, :] = (hat * vec[GAIN1 : GAIN1 + 1] + vec[BIAS1 : BIAS1 + 1]).astype(BF)
    for i in range(2):
        at = slice(i * 256, (i + 1) * 256)
        qkv = (dot(a1_ref[at, :], w) + bias).astype(BF)
        q_ref[at, :] = qkv[:, 384:]
        for j in range(4):
            kv_ref[j, at, :] = qkv[:, :384]


def project(c, rows, own, other, heads, perm_t):
    half = pl.BlockSpec((D // 2, COLS), lambda i: (0, 0))
    return pl.pallas_call(
        project_kernel,
        grid=(1,),
        in_specs=[
            pl.BlockSpec(memory_space=pltpu.SMEM),
            pl.BlockSpec((TP, TOK, D), lambda i: (0, 0, 0)),
            half,
            half,
            pl.BlockSpec((COLS, D), lambda i: (0, 0)),
            pl.BlockSpec((HW, D), lambda i: (0, 0)),
        ],
        out_specs=[
            pl.BlockSpec((ROWS, D), lambda i: (0, 0)),
            pl.BlockSpec((4, ROWS, 384), lambda i: (0, 0, 0)),
            pl.BlockSpec((ROWS, 384), lambda i: (0, 0)),
            pl.BlockSpec((16, D), lambda i: (0, 0)),
            pl.BlockSpec((D, COLS), lambda i: (0, 0)),
        ],
        out_shape=[
            shape((ROWS, D)),
            shape((4, ROWS, 384)),
            shape((ROWS, 384)),
            shape((16, D), F32),
            shape((D, COLS)),
        ],
        name="project",
        **settings(2_000_000_000),
    )(c, rows, own, other, heads, perm_t)


def feed_kernel(
    x_ref,
    o_ref,
    rows_ref,
    perm_ref,
    w_ref,
    vec_ref,
    da2_ref,
    act_ref,
    a2_ref,
    du_ref,
    resid_ref,
    op_ref,
    resid_s,
):
    vec = vec_ref[...]
    for i in range(2):
        at = slice(i * 256, (i + 1) * 256)
        op = None
        for j in range(TP):
            first = o_ref[j, :, 2 * i * HW : (2 * i + 1) * HW]
            later = o_ref[j, :, (2 * i + 1) * HW : (2 * i + 2) * HW]
            part = dot(jnp.concatenate([first, later], 0), perm_ref[j * HW : (j + 1) * HW, :])
            op = part if op is None else op + part
        op = op.astype(BF)
        op_ref[at, :] = op
        tok = jnp.concatenate([rows_ref[2 * i, 0:TOK, :], rows_ref[2 * i + 1, 0:TOK, :]], 0)
        dy = jnp.concatenate([rows_ref[2 * i, TOK:, :], rows_ref[2 * i + 1, TOK:, :]], 0)
        resid = tok.astype(F32) + dot(op, w_ref[:, D : 2 * D]) + vec[BOUT : BOUT + 1]
        resid_s[at, :] = resid
        hat, _ = standardized(resid)
        a2 = (hat * vec[GAIN2 : GAIN2 + 1] + vec[BIAS2 : BIAS2 + 1]).astype(BF)
        a2_ref[at, :] = a2
        act, slope = gelu_pair(dot(a2, w_ref[:, 0:D]) + vec[BFC1 : BFC1 + 1])
        du = (dot_nt(dy, w_ref[:, 2 * D :]) * slope).astype(BF)
        du_ref[at, :] = du
        act_ref[at, :] = act.astype(BF)
        da2 = dot_nt(du, w_ref[:, 0:D]).astype(BF)
        da2_ref[2 * i] = da2[:TOK]
        da2_ref[2 * i + 1] = da2[TOK:]
    resid_ref[...] = resid_s[pl.ds(pl.multiple_of(x_ref[0] * TOK, TOK), TOK), :]


def feed(x, o, rows, perm, w, vec):
    whole = pl.BlockSpec(memory_space=pltpu.VMEM)
    return pl.pallas_call(
        feed_kernel,
        in_specs=[pl.BlockSpec(memory_space=pltpu.SMEM)] + [whole] * 5,
        out_specs=[whole] * 6,
        out_shape=[
            shape((TP, TOK, D)),
            shape((ROWS, D)),
            shape((ROWS, D)),
            shape((ROWS, D)),
            shape((TOK, D), F32),
            shape((ROWS, D)),
        ],
        scratch_shapes=[pltpu.VMEM((ROWS, D), F32)],
        name="feed",
        **settings(4_000_000_000),
    )(x, o, rows, perm, w, vec)


def feed_grads_kernel(
    rows_ref,
    perm_ref,
    perm_t_ref,
    heads_ref,
    wo_ref,
    w2_ref,
    act_ref,
    a2_ref,
    du_ref,
    gw_ref,
    mixed_ref,
    gb_ref,
    wo_pad_ref,
    dy_s,
):
    wo_t = dot(perm_t_ref[...], wo_ref[...]).astype(BF)
    wo_pad_ref[...] = dot_tn(heads_ref[...], wo_t).astype(BF)
    for i in range(TP):
        at = slice(i * TOK, (i + 1) * TOK)
        dy_s[at, :] = dot_nt(rows_ref[i, TOK:, :], perm_ref[...]).astype(BF)
    for i in range(3):
        at = slice(i * 256, (i + 1) * 256)
        gw_ref[at, 0:D] = dot_tn(a2_ref[:, at], du_ref[...])
        gw_ref[at, D:] = dot_tn(act_ref[:, at], dy_s[...])
    for i in range(2):
        at = slice(i * 256, (i + 1) * 256)
        mixed_ref[at, :] = dot(act_ref[at, :], w2_ref[...]).astype(BF)
    gb_ref[...] = jnp.broadcast_to(jnp.sum(du_ref[...].astype(F32), 0, keepdims=True), (8, D))


def feed_grads(rows, perm, perm_t, heads, w, act, a2, du):
    whole = pl.BlockSpec((ROWS, D), lambda i: (0, 0))
    return pl.pallas_call(
        feed_grads_kernel,
        grid=(1,),
        in_specs=[
            pl.BlockSpec((TP, 2 * TOK, D), lambda i: (0, 0, 0)),
            pl.BlockSpec((D, D), lambda i: (0, 0)),
            pl.BlockSpec((HW, D), lambda i: (0, 0)),
            pl.BlockSpec((HW, 384), lambda i: (2, 0)),
            pl.BlockSpec((D, D), lambda i: (0, 1)),
            pl.BlockSpec((D, D), lambda i: (0, 2)),
            whole,
            whole,
            whole,
        ],
        out_specs=[
            pl.BlockSpec((D, 2 * D), lambda i: (0, 0)),
            whole,
            pl.BlockSpec((8, D), lambda i: (0, 0)),
            pl.BlockSpec((384, D), lambda i: (0, 0)),
        ],
        out_shape=[shape((D, 2 * D), F32), shape((ROWS, D)), shape((8, D), F32), shape((384, D))],
        scratch_shapes=[pltpu.VMEM((ROWS, D), BF)],
        name="feed_grads",
        **settings(3_000_000_000),
    )(rows, perm, perm_t, heads, w, w, act, a2, du)


def norm2_kernel(da2_ref, resid_ref, dy_ref, vec_ref, dbr_ref, dresid_ref, sums_ref):
    da2 = da2_ref[0].astype(F32)
    for i in range(1, TP):
        da2 = da2 + da2_ref[i].astype(F32)
    hat, rstd = standardized(resid_ref[...])
    dy = dy_ref[...].astype(F32)
    dresid = dy + norm_back(da2 * vec_ref[GAIN2 : GAIN2 + 1, :], hat, rstd)
    dresid_ref[...] = dresid
    dbr = dresid.astype(BF)
    dbr_ref[...] = dbr
    sums_ref[0:1, :] = jnp.sum(dbr.astype(F32), 0, keepdims=True)
    sums_ref[1:2, :] = jnp.sum(da2 * hat, 0, keepdims=True)
    sums_ref[2:3, :] = jnp.sum(da2, 0, keepdims=True)
    sums_ref[3:4, :] = jnp.sum(dy, 0, keepdims=True)
    sums_ref[4:8, :] = jnp.zeros((4, D), F32)


def norm2(da2, resid, dy, vec):
    return pl.pallas_call(
        norm2_kernel,
        out_shape=[shape((TOK, D)), shape((TOK, D), F32), shape((8, D), F32)],
        name="norm2",
        **settings(100_000_000),
    )(da2, resid, dy, vec)


def early_kernel(dq_ref, heads_ref, a1_ref, perm_t_ref, op_ref, dbr_ref, dqn_ref, pack_ref):
    dq = dot_nt(dq_ref[...], heads_ref[0:256, 384:]).astype(BF)
    dqn_ref[...] = dq
    dbr_t = [dot_nt(dbr_ref[i], perm_t_ref[...]).astype(BF) for i in range(TP)]
    dbr_t = jnp.concatenate(dbr_t, 0)
    for i in range(3):
        at = slice(i * 256, (i + 1) * 256)
        pack_ref[at, 0:256] = dot_tn(a1_ref[:, at], dq).astype(BF)
        pack_ref[at, 256 : 256 + HW] = dot_tn(op_ref[:, at], dbr_t).astype(BF)
        pack_ref[at, 256 + HW :] = jnp.zeros((256, 64), BF)


def early(dq, heads, a1, perm_t, op, dbr):
    return pl.pallas_call(
        early_kernel,
        out_shape=[shape((ROWS, 256)), shape((D, 512))],
        name="early",
        **settings(1_000_000_000),
    )(dq, heads, a1, perm_t, op, dbr)


def grads_kernel(
    c_ref,
    dkv_ref,
    dqn_ref,
    early_ref,
    heads_ref,
    w_ref,
    a1_ref,
    rows_ref,
    perm_t_ref,
    gb_ref,
    sums_ref,
    da1_ref,
    own_ref,
    other_ref,
    g_s,
    dqkv_s,
    pack_ref,
):
    ones = jnp.zeros((1, D), F32)
    gain, bias = ones, ones
    for i in range(2):
        at = slice(i * 256, (i + 1) * 256)
        dkv = dkv_ref[0, at, :].astype(F32)
        for j in range(1, 4):
            dkv = dkv + dkv_ref[j, at, :].astype(F32)
        dqkv = dot_nt(dkv.astype(BF), heads_ref[:, :384]).astype(BF)
        dqkv_s[at, :] = dqkv
        dqkv_s[at, 0:128] = dqn_ref[at, 0:128]
        dqkv_s[at, 128:256] = dqkv[:, 128:256] + dqn_ref[at, 128:256]
        da1 = dot_nt(dqkv_s[at, :], w_ref[...])
        da1_ref[at, :] = da1.astype(BF)
        tok = jnp.concatenate([rows_ref[2 * i], rows_ref[2 * i + 1]], 0)
        hat, _ = standardized(tok.astype(F32))
        gain = gain + jnp.sum(da1 * hat, 0, keepdims=True)
        bias = bias + jnp.sum(da1, 0, keepdims=True)
    dsum = jnp.sum(dqkv_s[...].astype(F32), 0, keepdims=True).astype(BF)
    dsum = jnp.broadcast_to(dsum, (8, COLS))
    lanes = lax.broadcasted_iota(jnp.int32, (COLS, HW), 0)
    head = lax.broadcasted_iota(jnp.int32, (COLS, HW), 1)
    g_bq = dot(dot(dsum, (lanes == head).astype(BF)).astype(BF), perm_t_ref[...])
    g_bv = dot(dot(dsum, (lanes == head + 2 * HW).astype(BF)).astype(BF), perm_t_ref[...])
    g_s[...] = jnp.zeros((128, D), F32)
    g_s[64 + GAIN1 : 65 + GAIN1, :] = gain
    g_s[64 + BIAS1 : 65 + BIAS1, :] = bias
    g_s[64 + BQ : 65 + BQ, :] = g_bq[0:1]
    g_s[64 + BV : 65 + BV, :] = g_bv[0:1]
    g_s[64 + BOUT : 64 + BOUT + 4, :] = sums_ref[0:4, :]
    g_s[64 + BFC1 : 65 + BFC1, :] = gb_ref[0:1, :]
    pack_ref[:, 0:128] = early_ref[:, 0:128]
    pack_ref[:, COLS:] = early_ref[:, 256:]
    for i in range(3):
        at = slice(i * 256, (i + 1) * 256)
        g = dot_tn(a1_ref[:, at], dqkv_s[:, 128:])
        pack_ref[at, 128:512] = g[:, :384].astype(BF)
        pack_ref[at, 512:COLS] = (g[:, 384:] + g_s[:, at].T).astype(BF)
    c = c_ref[0]
    own_ref[...] = pack_ref[pl.ds(pl.multiple_of(c * (D // 2), D // 2), D // 2), :]
    other_ref[...] = pack_ref[pl.ds(pl.multiple_of((1 - c) * (D // 2), D // 2), D // 2), :]


def grads(c, dkv, dqn, pack, heads, w, a1, rows, perm_t, gb, sums):
    def whole(*dims):
        return pl.BlockSpec(dims, lambda i: (0,) * len(dims))

    return pl.pallas_call(
        grads_kernel,
        grid=(1,),
        in_specs=[
            pl.BlockSpec(memory_space=pltpu.SMEM),
            whole(4, ROWS, 384),
            whole(ROWS, 256),
            whole(D, 512),
            whole(COLS, 384),
            whole(D, COLS),
            whole(ROWS, D),
            whole(TP, TOK, D),
            whole(HW, D),
            whole(8, D),
            whole(8, D),
        ],
        out_specs=[whole(ROWS, D), whole(D // 2, 896), whole(D // 2, 896)],
        out_shape=[shape((ROWS, D)), shape((D // 2, 896)), shape((D // 2, 896))],
        scratch_shapes=[
            pltpu.VMEM((128, D), F32),
            pltpu.VMEM((ROWS, COLS), BF),
            pltpu.VMEM((D, 896), BF),
        ],
        name="grads",
        **settings(2_000_000_000),
    )(c, dkv, dqn, pack, heads, w, a1, rows, perm_t, gb, sums)


def exchange(v, axes):
    return lax.all_to_all(v, axes, 0, 0, tiled=True)


def spread(v, axes, n):
    return exchange(jnp.broadcast_to(v[None], (n,) + v.shape), axes)


def per_device(
    tokens,
    cotangent,
    block_map,
    ln1_gain,
    ln1_bias,
    w_qkv,
    b_query,
    b_value,
    w_out,
    b_out,
    ln2_gain,
    ln2_bias,
    w_fc1,
    b_fc1,
    w_fc2,
    b_fc2,
):
    perm = jnp.asarray(feature_matrix())
    heads = jnp.asarray(head_matrix())
    z, x, c = lax.axis_index("z"), lax.axis_index("x"), lax.axis_index("c")
    perm_t = lax.dynamic_slice_in_dim(perm, x * HW, HW, 0)

    maps = block_map.reshape(4, 4, 2, 2).transpose(2, 0, 1, 3)
    maps = jnp.where(c == 0, maps, maps[::-1])
    kpos = maps.reshape(-1)
    own = lax.dynamic_slice(maps[0], (z, 0, 0), (1, 4, 2)).reshape(-1)
    before = own[None, :] < own[:, None]
    rank = jnp.sum(before.astype(jnp.int32), 1)
    ordered = jnp.sum(jnp.where(rank[:, None] == jnp.arange(8)[None, :], own[:, None], 0), 0)
    qpos = (ordered[:, None] * BLK + jnp.arange(BLK, dtype=jnp.int32)[None, :]).reshape(1, -1)
    qpos = jnp.broadcast_to(qpos, (8, ROWS))

    own_rows = dot(jnp.concatenate([tokens[0], cotangent[0]], 0), perm).astype(BF)
    all_rows = lax.all_gather(own_rows, "x", axis=0)

    out_cols = dot(jnp.concatenate([w_out, w_fc2], 0), perm).astype(BF)
    vectors = (ln1_gain, ln1_bias, b_query, b_value, b_out, ln2_gain, ln2_bias, b_fc2)
    vectors = sum(jnp.pad(v, (6 * i, 42 - 6 * i)) for i, v in enumerate(vectors))
    vectors = jnp.pad(vectors.reshape(8, 6).T, ((0, 0), (0, 56)))
    qkv_cols = w_qkv.reshape(6, 3, TP, HW).transpose(2, 0, 1, 3).reshape(TP, 6, 3 * HW)
    fc1_cols = w_fc1.reshape(6, 16, TP, 2, 24).transpose(2, 0, 3, 1, 4).reshape(TP, 6, D)
    sent = jnp.concatenate(
        [
            qkv_cols,
            jnp.broadcast_to(vectors[None], (TP, 6, 64)),
            fc1_cols,
            jnp.broadcast_to(out_cols[None, :6], (TP, 6, D)),
        ],
        2,
    )
    got = exchange(sent, "x").reshape(24, -1)
    first = jnp.where(
        jnp.arange(COLS)[None, :] == 3 * HW + BFC1, b_fc1[:, None], got[:, :COLS]
    )
    first = spread(first, ("y", "z"), 16).reshape(D // 2, COLS)
    other = lax.ppermute(first, "c", SWAP)
    rest = jnp.concatenate([got[:, COLS:], out_cols[6:]], 1)
    other, rest = lax.optimization_barrier((other, rest))
    second = lax.all_gather(rest, G, axis=0, tiled=True)

    core = c.reshape(1)
    a1, kv, q, vec, w_heads = project(core, all_rows, first, other, heads, perm_t)
    kv = exchange(kv, "z").reshape(KEYS // 2, 384)
    other = lax.ppermute(kv, "c", SWAP)
    o, o_t, lse, kvs, kvt, qs = attend(kpos, rank, qpos, q, kv, other)
    o = lax.all_gather(o, "x", axis=0)
    da2_part, act, a2, du, resid, o_perm = feed(x.reshape(1), o, all_rows, perm, second, vec)
    g_feed, mixed_part, g_bfc1, wo_pad = feed_grads(
        all_rows, perm, perm_t, heads, second, act, a2, du
    )

    da2 = exchange(da2_part, "x")
    da2, g_feed = lax.optimization_barrier((da2, g_feed))
    dbr, dresid, sums = norm2(da2, resid, own_rows[TOK:], vec)
    r_feed = lax.psum_scatter(g_feed, G, scatter_dimension=0, tiled=True)
    dbr = lax.all_gather(dbr, "x", axis=0)
    dbr, mixed_part = lax.optimization_barrier((dbr, mixed_part))
    mixed_part = exchange(mixed_part.reshape(TP, TOK, D), "x")
    dkv, dkv_other, dq = attend_back(
        kpos, rank, qpos, qs, kvs, kvt, dbr.reshape(ROWS, D), wo_pad, o_t, lse
    )
    dkv_other, mixed_part = lax.optimization_barrier((dkv_other, mixed_part))
    dkv_other = lax.ppermute(dkv_other, "c", SWAP)
    mixed = jnp.sum(mixed_part.astype(F32), 0)
    mixed = (resid + mixed + vec[BFC2 : BFC2 + 1]).astype(BF)
    mixed = dot_nt(mixed, perm).astype(BF)
    dkv = (dkv.astype(F32) + dkv_other.astype(F32)).astype(BF).reshape(4, ROWS, 384)
    dkv = exchange(dkv, "z")
    dqn, pack = early(dq, heads, a1, perm_t, o_perm, dbr)
    da1_part, pack, pack_other = grads(
        core, dkv, dqn, pack, heads, w_heads, a1, all_rows, perm_t, g_bfc1, sums
    )
    da1_part, r_feed = lax.optimization_barrier((da1_part, r_feed))
    da1 = lax.psum_scatter(da1_part, "x", scatter_dimension=0, tiled=True)
    da1 = da1.astype(F32)
    hat1, rstd1 = standardized(own_rows[:TOK].astype(F32))
    dtok = (dresid + norm_back(da1 * vec[GAIN1 : GAIN1 + 1], hat1, rstd1)).astype(BF)
    dtok = dot_nt(dtok, perm).astype(BF)

    pack_other = lax.ppermute(pack_other, "c", SWAP)
    half = (pack.astype(F32) + pack_other.astype(F32)).astype(BF)
    mine = jnp.sum(exchange(half, ("y", "z")).reshape(16, 24, -1).astype(F32), 0)
    last = jnp.concatenate([mine[:, : COLS + HW], r_feed[:, :D]], 1).astype(BF)
    last, dtok = lax.optimization_barrier((last, dtok))
    last = exchange(last.reshape(TP, 6, -1), "x").astype(F32)
    r_qkv = last[:, :, : 3 * HW].reshape(TP, 6, 3, HW).transpose(1, 2, 0, 3).reshape(6, 3 * D)
    r_out = last[:, :, COLS : COLS + HW].transpose(1, 0, 2).reshape(6, D)
    r_fc1 = last[:, :, COLS + HW :].reshape(TP, 6, 2, 16, 24)
    r_fc1 = r_fc1.transpose(1, 3, 0, 2, 4).reshape(6, FF)
    r_vec = jnp.sum(last[:, :, 3 * HW : 3 * HW + 8], 0)
    return (
        mixed[None],
        dtok[None],
        r_vec[:, GAIN1],
        r_vec[:, BIAS1],
        r_qkv,
        r_vec[:, BQ],
        r_vec[:, BV],
        r_out,
        r_vec[:, BOUT],
        r_vec[:, GAIN2],
        r_vec[:, BIAS2],
        r_fc1,
        mine[:, 3 * HW + BFC1],
        r_feed[:, D:],
        r_vec[:, BFC2],
    )


def solution(mesh):
    fine = Mesh(mesh.devices.reshape(4, 4, 4, 2), ("y", "z", "x", "c"))
    rows = P("y", ("z", "x", "c"), None)
    every = ("y", "z", "x", "c")
    vec, mat = P(every), P(every, None)
    in_specs = (rows, rows, P(), vec, vec, mat, vec, vec, mat, vec, vec, vec, mat, vec, mat, vec)
    out_specs = (rows, rows, vec, vec, mat, vec, vec, mat, vec, vec, vec, mat, vec, mat, vec)
    return jax.shard_map(
        per_device, mesh=fine, in_specs=in_specs, out_specs=out_specs, check_vma=False
    )
```

```python
import jax
import jax.numpy as jnp
import numpy as np
from jax import lax
from jax.experimental import pallas as pl
from jax.experimental.pallas import tpu as pltpu
from jax.sharding import Mesh, PartitionSpec as P

D = 768
H = 12
HD = 64
FF = 3072
BLK = 64
TP = 4
HL = H // TP
HW = HL * HD
COLS = 640
TOK = 128
ROWS = TOK * TP
KEYS = 4096
CHUNK = 1024
BACK = 2048
EPS = 1e-05
MASKED = -1e30
LOG2E = 1.4426950408889634
SCALE = HD**-0.5
BF = jnp.bfloat16
F32 = jnp.float32
G = ("c", "y", "z")
SWAP = ((0, 1), (1, 0))


def natural_feature(i):
    c, y, z, x, r = i // 384, (i // 96) % 4, (i // 24) % 4, (i // 6) % 4, i % 6
    return y * 192 + z * 48 + x * 12 + c * 6 + r


def feature_matrix():
    out = np.zeros((D, D), np.float32)
    i = np.arange(D)
    out[natural_feature(i), i] = 1
    return out.astype(jnp.bfloat16)


def head_matrix():
    out = np.zeros((COLS, 6 * 2 * HD), np.float32)
    for h in range(HL):
        for d in range(HD):
            out[HW + h * HD + d, h * 128 + d] = 1
            out[2 * HW + h * HD + d, h * 128 + HD + d] = 1
            out[h * HD + d, 384 + h * 128 + d] = 1
    return out.astype(jnp.bfloat16)


def place_matrix():
    out = np.zeros((2 * HW, 384), np.float32)
    for h in range(HL):
        for d in range(HD):
            out[HW + h * HD + d, h * 128 + HD + d] = 1
    return out.astype(jnp.bfloat16)


def dot(a, b):
    return lax.dot_general(a, b, (((1,), (0,)), ((), ())), preferred_element_type=F32)


def dot_nt(a, b):
    return lax.dot_general(a, b, (((1,), (1,)), ((), ())), preferred_element_type=F32)


def dot_tn(a, b):
    return lax.dot_general(a, b, (((0,), (0,)), ((), ())), preferred_element_type=F32)


def standardized(v):
    mean = jnp.mean(v, -1, keepdims=True)
    centered = v - mean
    rstd = lax.rsqrt(jnp.mean(centered * centered, -1, keepdims=True) + EPS)
    return centered * rstd, rstd


def norm_back(g, xhat, rstd):
    return rstd * (
        g - jnp.mean(g, -1, keepdims=True) - xhat * jnp.mean(g * xhat, -1, keepdims=True)
    )


def gelu_pair(u):
    k = 0.7978845608028654
    t = jnp.tanh(k * (u + 0.044715 * u * u * u))
    value = 0.5 * u * (1 + t)
    slope = 0.5 * (1 + t) + 0.5 * u * (1 - t * t) * k * (1 + 3 * 0.044715 * u * u)
    return value, slope


TILES = ((0, KEYS // 2), (ROWS // 2, KEYS))


def scores_t(kv, q, qpos, start, masked):
    s = dot_nt(kv, q)
    if masked:
        key = lax.broadcasted_iota(jnp.int32, s.shape, 0) + start
        s = jnp.where(key <= qpos, s, MASKED)
    return s


def attend_kernel(
    kpos, rank, qpos_ref, q_ref, own_ref, other_ref, o_ref, ot_ref, lse_ref, kvs_ref, kvt_ref, qs_ref, o_s, o_r
):
    head = pl.program_id(0)
    for b in range(KEYS // BLK):
        at = pl.multiple_of(kpos[b] * BLK, BLK)
        part = own_ref if b < KEYS // BLK // 2 else other_ref
        row = b % (KEYS // BLK // 2) * BLK
        kvs_ref[pl.ds(at, BLK), :] = part[row : row + BLK, :]
    for b in range(ROWS // BLK):
        at = pl.multiple_of(rank[b] * BLK, BLK)
        qs_ref[pl.ds(at, BLK), :] = q_ref[b * BLK : (b + 1) * BLK, :] * SCALE
    for i in range(KEYS // CHUNK):
        kvt_ref[:, i * CHUNK : (i + 1) * CHUNK] = kvs_ref[i * CHUNK : (i + 1) * CHUNK, :].T
    for first, span in TILES:
        q = qs_ref[first : first + 256, :]
        qpos = qpos_ref[0:1, first : first + 256]
        top = jnp.full((8, 256), MASKED, F32)
        for start in range(0, span, CHUNK):
            masked = start + CHUNK > span - KEYS // 2
            s = scores_t(kvs_ref[start : start + CHUNK, :], q, qpos, start, masked)
            top = jnp.maximum(top, jnp.max(s.reshape(-1, 8, 256), 0))
        top = jnp.max(top, 0, keepdims=True) * LOG2E
        mass = jnp.zeros((8, 256), F32)
        acc = jnp.zeros((128, 256), F32)
        for start in range(0, span, CHUNK):
            masked = start + CHUNK > span - KEYS // 2
            s = scores_t(kvs_ref[start : start + CHUNK, :], q, qpos, start, masked)
            p = jnp.exp2(s * LOG2E - top)
            mass = mass + jnp.sum(p.reshape(-1, 8, 256), 0)
            acc = acc + dot(kvt_ref[:, start : start + CHUNK], p.astype(BF))
        mass = jnp.sum(mass, 0, keepdims=True)
        o = acc[HD:, :] * (1.0 / mass)
        ot_ref[:, first : first + 256] = o
        o_s[pl.ds(pl.multiple_of(head * HD, HD), HD), first : first + 256] = o
        lse_ref[0, :, first : first + 256] = jnp.broadcast_to(top + jnp.log2(mass), (8, 256))

    @pl.when(head == HL - 1)
    def _():
        o_r[...] = o_s[...].T.astype(BF)
        for b in range(ROWS // BLK):
            at = pl.multiple_of(rank[b] * BLK, BLK)
            row, col = b * BLK % TOK, b * BLK // TOK * HW
            o_ref[row : row + BLK, col : col + HW] = o_r[pl.ds(at, BLK), :]


def attend_back_kernel(
    kpos,
    rank,
    qpos_ref,
    qs_ref,
    kvs_ref,
    kvt_ref,
    dbr_ref,
    place_ref,
    o_ref,
    lse_ref,
    own_ref,
    other_ref,
    dq_ref,
    dos,
    acc,
):
    do_all = dot(dbr_ref[...], place_ref[...]).astype(BF)
    for b in range(ROWS // BLK):
        at = pl.multiple_of(rank[b] * BLK, BLK)
        dos[pl.ds(at, BLK), :] = do_all[b * BLK : (b + 1) * BLK, :]
    dot_t = dos[...].astype(F32).T
    delta = jnp.sum(dot_t[HD:, :] * o_ref[...], 0, keepdims=True)
    dq = [jnp.zeros((128, 256), F32), jnp.zeros((128, 256), F32)]
    for start in range(0, KEYS, BACK):
        kv = kvs_ref[start : start + BACK, :]
        kvt = kvt_ref[:, start : start + BACK]
        total = None
        for n, (first, span) in enumerate(TILES):
            if start >= span:
                continue
            cols = slice(first, first + 256)
            q = qs_ref[cols, :]
            do = dos[cols, :]
            s = scores_t(kv, q, qpos_ref[0:1, cols], start, start + BACK > span - KEYS // 2)
            p = jnp.exp2(s * LOG2E - lse_ref[0, 0:1, cols])
            dp = dot_nt(kv, do)
            ds = (p * (dp - delta[:, cols])).astype(BF)
            part = dot(ds, q) + dot(p.astype(BF), do)
            total = part if total is None else total + part
            dq[n] = dq[n] + dot(kvt, ds)
        acc[start : start + BACK, :] = total.astype(BF)
    for b in range(KEYS // BLK):
        at = pl.multiple_of(kpos[b] * BLK, BLK)
        part = own_ref if b < KEYS // BLK // 2 else other_ref
        row = b % (KEYS // BLK // 2) * BLK
        part[row : row + BLK, :] = acc[pl.ds(at, BLK), :]
    dos[0:256, :] = (dq[0] * SCALE).T.astype(BF)
    dos[256:512, :] = (dq[1] * SCALE).T.astype(BF)
    for b in range(ROWS // BLK):
        at = pl.multiple_of(rank[b] * BLK, BLK)
        dq_ref[b * BLK : (b + 1) * BLK, :] = dos[pl.ds(at, BLK), :]


def settings(flops):
    return dict(
        compiler_params=pltpu.CompilerParams(vmem_limit_bytes=56 * 1024 * 1024),
        cost_estimate=pl.CostEstimate(flops=flops, bytes_accessed=8_000_000, transcendentals=0),
    )


def shape(dims, kind=BF):
    return jax.ShapeDtypeStruct(dims, kind)


def attend(kpos, rank, qpos, q, own, other):
    grid_spec = pltpu.PrefetchScalarGridSpec(
        num_scalar_prefetch=2,
        grid=(HL,),
        in_specs=[
            pl.BlockSpec((8, ROWS), lambda h, *_: (0, 0)),
            pl.BlockSpec((ROWS, 128), lambda h, *_: (0, h)),
            pl.BlockSpec((KEYS // 2, 128), lambda h, *_: (0, h)),
            pl.BlockSpec((KEYS // 2, 128), lambda h, *_: (0, h)),
        ],
        out_specs=[
            pl.BlockSpec((TOK, D), lambda h, *_: (0, 0)),
            pl.BlockSpec((HD, ROWS), lambda h, *_: (h, 0)),
            pl.BlockSpec((1, 8, ROWS), lambda h, *_: (h, 0, 0)),
            pl.BlockSpec((KEYS, 128), lambda h, *_: (0, h)),
            pl.BlockSpec((128, KEYS), lambda h, *_: (h, 0)),
            pl.BlockSpec((ROWS, 128), lambda h, *_: (0, h)),
        ],
        scratch_shapes=[pltpu.VMEM((HW, ROWS), F32), pltpu.VMEM((ROWS, HW), BF)],
    )
    return pl.pallas_call(
        attend_kernel,
        grid_spec=grid_spec,
        out_shape=[
            shape((TOK, D)),
            shape((HW, ROWS), F32),
            shape((HL, 8, ROWS), F32),
            shape((KEYS, 384)),
            shape((384, KEYS)),
            shape((ROWS, 384)),
        ],
        name="attend",
        **settings(5_000_000_000),
    )(kpos, rank, qpos, q, own, other)


def attend_back(kpos, rank, qpos, qs, kvs, kvt, dbr, place, o, lse):
    grid_spec = pltpu.PrefetchScalarGridSpec(
        num_scalar_prefetch=2,
        grid=(HL,),
        in_specs=[
            pl.BlockSpec((8, ROWS), lambda h, *_: (0, 0)),
            pl.BlockSpec((ROWS, 128), lambda h, *_: (0, h)),
            pl.BlockSpec((KEYS, 128), lambda h, *_: (0, h)),
            pl.BlockSpec((128, KEYS), lambda h, *_: (h, 0)),
            pl.BlockSpec((ROWS, 2 * HW), lambda h, *_: (0, 0)),
            pl.BlockSpec((2 * HW, 128), lambda h, *_: (0, h)),
            pl.BlockSpec((HD, ROWS), lambda h, *_: (h, 0)),
            pl.BlockSpec((1, 8, ROWS), lambda h, *_: (h, 0, 0)),
        ],
        out_specs=[
            pl.BlockSpec((KEYS // 2, 128), lambda h, *_: (0, h)),
            pl.BlockSpec((KEYS // 2, 128), lambda h, *_: (0, h)),
            pl.BlockSpec((ROWS, 128), lambda h, *_: (0, h)),
        ],
        scratch_shapes=[pltpu.VMEM((ROWS, 128), BF), pltpu.VMEM((KEYS, 128), BF)],
    )
    return pl.pallas_call(
        attend_back_kernel,
        grid_spec=grid_spec,
        out_shape=[shape((KEYS // 2, 384)), shape((KEYS // 2, 384)), shape((ROWS, 384))],
        name="attend_back",
        **settings(15_000_000_000),
    )(kpos, rank, qpos, qs, kvs, kvt, dbr, place, o, lse)


GAIN1, BIAS1, BQ, BV, BOUT, GAIN2, BIAS2, BFC2, BFC1 = range(9)


def project_kernel(
    c_ref, rows_ref, own_ref, other_ref, heads_ref, perm_t_ref, a1_ref, kv_ref, q_ref, vec_ref, w_ref
):
    c = c_ref[0]
    w_ref[pl.ds(pl.multiple_of(c * (D // 2), D // 2), D // 2), :] = own_ref[...]
    w_ref[pl.ds(pl.multiple_of((1 - c) * (D // 2), D // 2), D // 2), :] = other_ref[...]
    vec = w_ref[:, 512:].astype(F32).T[64:80]
    vec_ref[...] = vec
    bqv = dot_nt(vec[0:8].astype(BF), perm_t_ref[...]).astype(BF)
    bias = (
        dot(bqv, heads_ref[0:HW, :])[BQ : BQ + 1]
        + dot(bqv, heads_ref[2 * HW : 3 * HW, :])[BV : BV + 1]
    )
    w = dot(w_ref[...], heads_ref[...]).astype(BF)
    for i in range(TP):
        at = slice(i * TOK, (i + 1) * TOK)
        hat, _ = standardized(rows_ref[i, 0:TOK, :].astype(F32))
        a1_ref[at, :] = (hat * vec[GAIN1 : GAIN1 + 1] + vec[BIAS1 : BIAS1 + 1]).astype(BF)
    for i in range(2):
        at = slice(i * 256, (i + 1) * 256)
        qkv = (dot(a1_ref[at, :], w) + bias).astype(BF)
        q_ref[at, :] = qkv[:, 384:]
        for j in range(4):
            kv_ref[j, at, :] = qkv[:, :384]


def project(c, rows, own, other, heads, perm_t):
    half = pl.BlockSpec((D // 2, COLS), lambda i: (0, 0))
    return pl.pallas_call(
        project_kernel,
        grid=(1,),
        in_specs=[
            pl.BlockSpec(memory_space=pltpu.SMEM),
            pl.BlockSpec((TP, TOK, D), lambda i: (0, 0, 0)),
            half,
            half,
            pl.BlockSpec((COLS, D), lambda i: (0, 0)),
            pl.BlockSpec((HW, D), lambda i: (0, 0)),
        ],
        out_specs=[
            pl.BlockSpec((ROWS, D), lambda i: (0, 0)),
            pl.BlockSpec((4, ROWS, 384), lambda i: (0, 0, 0)),
            pl.BlockSpec((ROWS, 384), lambda i: (0, 0)),
            pl.BlockSpec((16, D), lambda i: (0, 0)),
            pl.BlockSpec((D, COLS), lambda i: (0, 0)),
        ],
        out_shape=[
            shape((ROWS, D)),
            shape((4, ROWS, 384)),
            shape((ROWS, 384)),
            shape((16, D), F32),
            shape((D, COLS)),
        ],
        name="project",
        **settings(2_000_000_000),
    )(c, rows, own, other, heads, perm_t)


def feed_kernel(
    x_ref,
    o_ref,
    rows_ref,
    perm_ref,
    w_ref,
    vec_ref,
    da2_ref,
    act_ref,
    a2_ref,
    du_ref,
    resid_ref,
    op_ref,
    resid_s,
    w_s,
    sems,
):
    copies = [
        pltpu.make_async_copy(w_ref.at[:, pl.ds(i * D, D)], w_s.at[i], sems.at[i]) for i in range(3)
    ]
    for i in (1, 0, 2):
        copies[i].start()
    vec = vec_ref[...]
    for i in range(2):
        at = slice(i * 256, (i + 1) * 256)
        op = None
        for j in range(TP):
            first = o_ref[j, :, 2 * i * HW : (2 * i + 1) * HW]
            later = o_ref[j, :, (2 * i + 1) * HW : (2 * i + 2) * HW]
            part = dot(jnp.concatenate([first, later], 0), perm_ref[j * HW : (j + 1) * HW, :])
            op = part if op is None else op + part
        op = op.astype(BF)
        op_ref[at, :] = op
        tok = jnp.concatenate([rows_ref[2 * i, 0:TOK, :], rows_ref[2 * i + 1, 0:TOK, :]], 0)
        dy = jnp.concatenate([rows_ref[2 * i, TOK:, :], rows_ref[2 * i + 1, TOK:, :]], 0)
        if i == 0:
            copies[1].wait()
        resid = tok.astype(F32) + dot(op, w_s[1]) + vec[BOUT : BOUT + 1]
        resid_s[at, :] = resid
        hat, _ = standardized(resid)
        a2 = (hat * vec[GAIN2 : GAIN2 + 1] + vec[BIAS2 : BIAS2 + 1]).astype(BF)
        a2_ref[at, :] = a2
        if i == 0:
            copies[0].wait()
        act, slope = gelu_pair(dot(a2, w_s[0]) + vec[BFC1 : BFC1 + 1])
        if i == 0:
            copies[2].wait()
        du = (dot_nt(dy, w_s[2]) * slope).astype(BF)
        du_ref[at, :] = du
        act_ref[at, :] = act.astype(BF)
        da2 = dot_nt(du, w_s[0]).astype(BF)
        da2_ref[2 * i] = da2[:TOK]
        da2_ref[2 * i + 1] = da2[TOK:]
    resid_ref[...] = resid_s[pl.ds(pl.multiple_of(x_ref[0] * TOK, TOK), TOK), :]


def feed(x, o, rows, perm, w, vec):
    whole = pl.BlockSpec(memory_space=pltpu.VMEM)
    return pl.pallas_call(
        feed_kernel,
        in_specs=[pl.BlockSpec(memory_space=pltpu.SMEM)]
        + [whole] * 3
        + [pl.BlockSpec(memory_space=pl.ANY), whole],
        out_specs=[whole] * 6,
        out_shape=[
            shape((TP, TOK, D)),
            shape((ROWS, D)),
            shape((ROWS, D)),
            shape((ROWS, D)),
            shape((TOK, D), F32),
            shape((ROWS, D)),
        ],
        scratch_shapes=[
            pltpu.VMEM((ROWS, D), F32),
            pltpu.VMEM((3, D, D), BF),
            pltpu.SemaphoreType.DMA((3,)),
        ],
        name="feed",
        **settings(4_000_000_000),
    )(x, o, rows, perm, w, vec)


def feed_grads_kernel(
    rows_ref,
    perm_ref,
    w2_ref,
    act_ref,
    a2_ref,
    du_ref,
    gw_ref,
    mixed_ref,
    gb_ref,
    dy_s,
):
    for i in range(TP):
        at = slice(i * TOK, (i + 1) * TOK)
        dy_s[at, :] = dot_nt(rows_ref[i, TOK:, :], perm_ref[...]).astype(BF)
    for core in range(2):
        at = slice(core * 384, (core + 1) * 384)
        g_fc1 = dot_tn(a2_ref[:, at], du_ref[...]).astype(BF)
        g_fc2 = dot_tn(act_ref[:, at], dy_s[...]).astype(BF)
        for y in range(4):
            to = slice(y * 192 + core * 96, y * 192 + (core + 1) * 96)
            gw_ref[to, 0:D] = g_fc1[y * 96 : (y + 1) * 96]
            gw_ref[to, D:] = g_fc2[y * 96 : (y + 1) * 96]
    for i in range(2):
        at = slice(i * 256, (i + 1) * 256)
        mixed_ref[at, :] = dot(act_ref[at, :], w2_ref[...]).astype(BF)
    gb_ref[...] = jnp.broadcast_to(jnp.sum(du_ref[...].astype(F32), 0, keepdims=True), (8, D))


def feed_grads(rows, perm, w, act, a2, du):
    whole = pl.BlockSpec((ROWS, D), lambda i: (0, 0))
    return pl.pallas_call(
        feed_grads_kernel,
        grid=(1,),
        in_specs=[
            pl.BlockSpec((TP, 2 * TOK, D), lambda i: (0, 0, 0)),
            pl.BlockSpec((D, D), lambda i: (0, 0)),
            pl.BlockSpec((D, D), lambda i: (0, 2)),
            whole,
            whole,
            whole,
        ],
        out_specs=[
            pl.BlockSpec((D, 2 * D), lambda i: (0, 0)),
            whole,
            pl.BlockSpec((8, D), lambda i: (0, 0)),
        ],
        out_shape=[shape((D, 2 * D)), shape((ROWS, D)), shape((8, D), F32)],
        scratch_shapes=[pltpu.VMEM((ROWS, D), BF)],
        name="feed_grads",
        **settings(3_000_000_000),
    )(rows, perm, w, act, a2, du)


def norm2_kernel(
    da2_ref, resid_ref, dy_ref, vec_ref, wo_ref, perm_ref, send_ref, dresid_ref, sums_ref
):
    da2 = da2_ref[0].astype(F32)
    for i in range(1, TP):
        da2 = da2 + da2_ref[i].astype(F32)
    hat, rstd = standardized(resid_ref[...])
    dy = dy_ref[...].astype(F32)
    dresid = dy + norm_back(da2 * vec_ref[GAIN2 : GAIN2 + 1, :], hat, rstd)
    dresid_ref[...] = dresid
    dbr = dresid.astype(BF)
    do = dot_nt(dbr, wo_ref[...]).astype(BF)
    dbr_nat = dot_nt(dbr, perm_ref[...]).astype(BF)
    do_nat = dot_nt(do, perm_ref[...]).astype(BF)
    for i in range(TP):
        send_ref[i, :, 0:HW] = dbr_nat[:, i * HW : (i + 1) * HW]
        send_ref[i, :, HW:] = do_nat[:, i * HW : (i + 1) * HW]
    sums_ref[0:1, :] = jnp.sum(dbr.astype(F32), 0, keepdims=True)
    sums_ref[1:2, :] = jnp.sum(da2 * hat, 0, keepdims=True)
    sums_ref[2:3, :] = jnp.sum(da2, 0, keepdims=True)
    sums_ref[3:4, :] = jnp.sum(dy, 0, keepdims=True)
    sums_ref[4:8, :] = jnp.zeros((4, D), F32)


def norm2(da2, resid, dy, vec, w, perm):
    def whole(*dims):
        return pl.BlockSpec(dims, lambda i: (0,) * len(dims))

    return pl.pallas_call(
        norm2_kernel,
        grid=(1,),
        in_specs=[
            whole(TP, TOK, D),
            whole(TOK, D),
            pl.BlockSpec((TOK, D), lambda i: (1, 0)),
            whole(16, D),
            pl.BlockSpec((D, D), lambda i: (0, 1)),
            whole(D, D),
        ],
        out_specs=[whole(TP, TOK, 2 * HW), whole(TOK, D), whole(8, D)],
        out_shape=[shape((TP, TOK, 2 * HW)), shape((TOK, D), F32), shape((8, D), F32)],
        name="norm2",
        **settings(100_000_000),
    )(da2, resid, dy, vec, w, perm)


def early_kernel(dq_ref, heads_ref, a1_ref, op_ref, dbr_ref, dqn_ref, pack_ref):
    dq = dot_nt(dq_ref[...], heads_ref[0:256, 384:]).astype(BF)
    dqn_ref[...] = dq
    dbr_t = dbr_ref[:, 0:HW]
    for i in range(3):
        at = slice(i * 256, (i + 1) * 256)
        pack_ref[at, 0:256] = dot_tn(a1_ref[:, at], dq).astype(BF)
        pack_ref[at, 256 : 256 + HW] = dot_tn(op_ref[:, at], dbr_t).astype(BF)
        pack_ref[at, 256 + HW :] = jnp.zeros((256, 64), BF)


def early(dq, heads, a1, op, dbr):
    return pl.pallas_call(
        early_kernel,
        out_shape=[shape((ROWS, 256)), shape((D, 512))],
        name="early",
        **settings(1_000_000_000),
    )(dq, heads, a1, op, dbr)


def grads_kernel(
    c_ref,
    dkv_ref,
    dqn_ref,
    early_ref,
    heads_ref,
    w_ref,
    a1_ref,
    rows_ref,
    perm_t_ref,
    gb_ref,
    sums_ref,
    da1_ref,
    own_ref,
    other_ref,
    g_s,
    dqkv_s,
    pack_ref,
):
    ones = jnp.zeros((1, D), F32)
    gain, bias = ones, ones
    for i in range(2):
        at = slice(i * 256, (i + 1) * 256)
        dkv = dkv_ref[0, at, :].astype(F32)
        for j in range(1, 4):
            dkv = dkv + dkv_ref[j, at, :].astype(F32)
        dqkv = dot_nt(dkv.astype(BF), heads_ref[:, :384]).astype(BF)
        dqkv_s[at, :] = dqkv
        dqkv_s[at, 0:128] = dqn_ref[at, 0:128]
        dqkv_s[at, 128:256] = dqkv[:, 128:256] + dqn_ref[at, 128:256]
        da1 = dot_nt(dqkv_s[at, :], w_ref[...])
        da1_ref[at, :] = da1.astype(BF)
        tok = jnp.concatenate([rows_ref[2 * i], rows_ref[2 * i + 1]], 0)
        hat, _ = standardized(tok.astype(F32))
        gain = gain + jnp.sum(da1 * hat, 0, keepdims=True)
        bias = bias + jnp.sum(da1, 0, keepdims=True)
    dsum = jnp.sum(dqkv_s[...].astype(F32), 0, keepdims=True).astype(BF)
    dsum = jnp.broadcast_to(dsum, (8, COLS))
    lanes = lax.broadcasted_iota(jnp.int32, (COLS, HW), 0)
    head = lax.broadcasted_iota(jnp.int32, (COLS, HW), 1)
    g_bq = dot(dot(dsum, (lanes == head).astype(BF)).astype(BF), perm_t_ref[...])
    g_bv = dot(dot(dsum, (lanes == head + 2 * HW).astype(BF)).astype(BF), perm_t_ref[...])
    g_s[...] = jnp.zeros((128, D), F32)
    g_s[64 + GAIN1 : 65 + GAIN1, :] = gain
    g_s[64 + BIAS1 : 65 + BIAS1, :] = bias
    g_s[64 + BQ : 65 + BQ, :] = g_bq[0:1]
    g_s[64 + BV : 65 + BV, :] = g_bv[0:1]
    g_s[64 + BOUT : 64 + BOUT + 4, :] = sums_ref[0:4, :]
    g_s[64 + BFC1 : 65 + BFC1, :] = gb_ref[0:1, :]
    pack_ref[:, 0:128] = early_ref[:, 0:128]
    pack_ref[:, COLS:] = early_ref[:, 256:]
    for i in range(3):
        at = slice(i * 256, (i + 1) * 256)
        g = dot_tn(a1_ref[:, at], dqkv_s[:, 128:])
        pack_ref[at, 128:512] = g[:, :384].astype(BF)
        pack_ref[at, 512:COLS] = (g[:, 384:] + g_s[:, at].T).astype(BF)
    c = c_ref[0]
    own_ref[...] = pack_ref[pl.ds(pl.multiple_of(c * (D // 2), D // 2), D // 2), :]
    other_ref[...] = pack_ref[pl.ds(pl.multiple_of((1 - c) * (D // 2), D // 2), D // 2), :]


def grads(c, dkv, dqn, pack, heads, w, a1, rows, perm_t, gb, sums):
    def whole(*dims):
        return pl.BlockSpec(dims, lambda i: (0,) * len(dims))

    return pl.pallas_call(
        grads_kernel,
        grid=(1,),
        in_specs=[
            pl.BlockSpec(memory_space=pltpu.SMEM),
            whole(4, ROWS, 384),
            whole(ROWS, 256),
            whole(D, 512),
            whole(COLS, 384),
            whole(D, COLS),
            whole(ROWS, D),
            whole(TP, TOK, D),
            whole(HW, D),
            whole(8, D),
            whole(8, D),
        ],
        out_specs=[whole(ROWS, D), whole(D // 2, 896), whole(D // 2, 896)],
        out_shape=[shape((ROWS, D)), shape((D // 2, 896)), shape((D // 2, 896))],
        scratch_shapes=[
            pltpu.VMEM((128, D), F32),
            pltpu.VMEM((ROWS, COLS), BF),
            pltpu.VMEM((D, 896), BF),
        ],
        name="grads",
        **settings(2_000_000_000),
    )(c, dkv, dqn, pack, heads, w, a1, rows, perm_t, gb, sums)


def exchange(v, axes):
    return lax.all_to_all(v, axes, 0, 0, tiled=True)


def spread(v, axes, n):
    return exchange(jnp.broadcast_to(v[None], (n,) + v.shape), axes)


def per_device(
    tokens,
    cotangent,
    block_map,
    ln1_gain,
    ln1_bias,
    w_qkv,
    b_query,
    b_value,
    w_out,
    b_out,
    ln2_gain,
    ln2_bias,
    w_fc1,
    b_fc1,
    w_fc2,
    b_fc2,
):
    perm = jnp.asarray(feature_matrix())
    heads = jnp.asarray(head_matrix())
    z, x, c = lax.axis_index("z"), lax.axis_index("x"), lax.axis_index("c")
    perm_t = lax.dynamic_slice_in_dim(perm, x * HW, HW, 0)

    maps = block_map.reshape(4, 4, 2, 2).transpose(2, 0, 1, 3)
    maps = jnp.where(c == 0, maps, maps[::-1])
    kpos = maps.reshape(-1)
    own = lax.dynamic_slice(maps[0], (z, 0, 0), (1, 4, 2)).reshape(-1)
    before = own[None, :] < own[:, None]
    rank = jnp.sum(before.astype(jnp.int32), 1)
    ordered = jnp.sum(jnp.where(rank[:, None] == jnp.arange(8)[None, :], own[:, None], 0), 0)
    qpos = (ordered[:, None] * BLK + jnp.arange(BLK, dtype=jnp.int32)[None, :]).reshape(1, -1)
    qpos = jnp.broadcast_to(qpos, (8, ROWS))

    out_cols = dot(jnp.concatenate([w_out, w_fc2], 0), perm).astype(BF)
    vectors = (ln1_gain, ln1_bias, b_query, b_value, b_out, ln2_gain, ln2_bias, b_fc2)
    vectors = sum(jnp.pad(v, (6 * i, 42 - 6 * i)) for i, v in enumerate(vectors))
    vectors = jnp.pad(vectors.reshape(8, 6).T, ((0, 0), (0, 56)))
    qkv_cols = w_qkv.reshape(6, 3, TP, HW).transpose(2, 0, 1, 3).reshape(TP, 6, 3 * HW)
    fc1_cols = w_fc1.reshape(6, 16, TP, 2, 24).transpose(2, 0, 3, 1, 4).reshape(TP, 6, D)
    sent = jnp.concatenate(
        [
            qkv_cols,
            jnp.broadcast_to(vectors[None], (TP, 6, 64)),
            fc1_cols,
            jnp.broadcast_to(out_cols[None, :6], (TP, 6, D)),
        ],
        2,
    )
    both = jnp.concatenate([tokens[0], cotangent[0]], 0)
    own_rows = dot(both, perm).astype(BF)
    all_rows = lax.all_gather(own_rows, "x", axis=0)

    got = exchange(sent, "x").reshape(24, -1)
    got, perm_t = lax.optimization_barrier((got, perm_t))
    first = jnp.where(
        jnp.arange(COLS)[None, :] == 3 * HW + BFC1, b_fc1[:, None], got[:, :COLS]
    )
    first = spread(first, ("y", "z"), 16).reshape(D // 2, COLS)
    other = lax.ppermute(first, "c", SWAP)
    rest = jnp.concatenate([got[:, COLS:], out_cols[6:]], 1)
    other, rest = lax.optimization_barrier((other, rest))
    second = lax.all_gather(rest, G, axis=0, tiled=True)

    core = c.reshape(1)
    a1, kv, q, vec, w_heads = project(core, all_rows, first, other, heads, perm_t)
    kv = exchange(kv, "z").reshape(KEYS // 2, 384)
    other = lax.ppermute(kv, "c", SWAP)
    o, o_t, lse, kvs, kvt, qs = attend(kpos, rank, qpos, q, kv, other)
    o = lax.all_gather(o, "x", axis=0)
    da2_part, act, a2, du, resid, o_perm = feed(x.reshape(1), o, all_rows, perm, second, vec)
    g_feed, mixed_part, g_bfc1 = feed_grads(all_rows, perm, second, act, a2, du)

    da2 = exchange(da2_part, "x")
    da2, g_feed = lax.optimization_barrier((da2, g_feed))
    dbr, dresid, sums = norm2(da2, resid, own_rows, vec, second, perm)
    r_feed = lax.psum_scatter(g_feed, "y", scatter_dimension=0, tiled=True)
    dbr = exchange(dbr, "x").reshape(ROWS, 2 * HW)
    dbr, mixed_part = lax.optimization_barrier((dbr, mixed_part))
    mixed_part = exchange(mixed_part.reshape(TP, TOK, D), "x")
    dkv, dkv_other, dq = attend_back(
        kpos, rank, qpos, qs, kvs, kvt, dbr, jnp.asarray(place_matrix()), o_t, lse
    )
    dkv_other, mixed_part, r_feed = lax.optimization_barrier((dkv_other, mixed_part, r_feed))
    r_feed = lax.psum_scatter(r_feed, ("c", "z"), scatter_dimension=0, tiled=True)
    dkv_other = lax.ppermute(dkv_other, "c", SWAP)
    mixed = jnp.sum(mixed_part.astype(F32), 0)
    mixed = (resid + mixed + vec[BFC2 : BFC2 + 1]).astype(BF)
    mixed = dot_nt(mixed, perm).astype(BF)
    dkv = (dkv.astype(F32) + dkv_other.astype(F32)).astype(BF).reshape(4, ROWS, 384)
    dkv = exchange(dkv, "z")
    dkv, r_feed = lax.optimization_barrier((dkv, r_feed))
    dqn, pack = early(dq, heads, a1, o_perm, dbr)
    da1_part, pack, pack_other = grads(
        core, dkv, dqn, pack, heads, w_heads, a1, all_rows, perm_t, g_bfc1, sums
    )
    da1 = lax.psum_scatter(da1_part, "x", scatter_dimension=0, tiled=True)
    da1 = da1.astype(F32)
    hat1, rstd1 = standardized(own_rows[:TOK].astype(F32))
    dtok = (dresid + norm_back(da1 * vec[GAIN1 : GAIN1 + 1], hat1, rstd1)).astype(BF)
    dtok = dot_nt(dtok, perm).astype(BF)

    r_feed = r_feed.astype(F32)
    pack_other = lax.ppermute(pack_other, "c", SWAP)
    half = (pack.astype(F32) + pack_other.astype(F32)).astype(BF)
    mine = jnp.sum(exchange(half, ("y", "z")).reshape(16, 24, -1).astype(F32), 0)
    last = jnp.concatenate([mine[:, : COLS + HW], r_feed[:, :D]], 1).astype(BF)
    last = exchange(last.reshape(TP, 6, -1), "x")
    last, dtok, mixed = lax.optimization_barrier((last, dtok, mixed))
    last = last.astype(F32)
    r_qkv = last[:, :, : 3 * HW].reshape(TP, 6, 3, HW).transpose(1, 2, 0, 3).reshape(6, 3 * D)
    r_out = last[:, :, COLS : COLS + HW].transpose(1, 0, 2).reshape(6, D)
    r_fc1 = last[:, :, COLS + HW :].reshape(TP, 6, 2, 16, 24)
    r_fc1 = r_fc1.transpose(1, 3, 0, 2, 4).reshape(6, FF)
    r_vec = jnp.sum(last[:, :, 3 * HW : 3 * HW + 8], 0)
    return (
        mixed[None],
        dtok[None],
        r_vec[:, GAIN1],
        r_vec[:, BIAS1],
        r_qkv,
        r_vec[:, BQ],
        r_vec[:, BV],
        r_out,
        r_vec[:, BOUT],
        r_vec[:, GAIN2],
        r_vec[:, BIAS2],
        r_fc1,
        mine[:, 3 * HW + BFC1],
        r_feed[:, D:],
        r_vec[:, BFC2],
    )


def solution(mesh):
    fine = Mesh(mesh.devices.reshape(4, 4, 4, 2), ("y", "z", "x", "c"))
    rows = P("y", ("z", "x", "c"), None)
    every = ("y", "z", "x", "c")
    vec, mat = P(every), P(every, None)
    in_specs = (rows, rows, P(), vec, vec, mat, vec, vec, mat, vec, vec, vec, mat, vec, mat, vec)
    out_specs = (rows, rows, vec, vec, mat, vec, vec, mat, vec, vec, vec, mat, vec, mat, vec)
    return jax.shard_map(
        per_device, mesh=fine, in_specs=in_specs, out_specs=out_specs, check_vma=False
    )
```

```python
import jax
import jax.numpy as jnp
import numpy as np
from jax import lax
from jax.experimental import pallas as pl
from jax.experimental.pallas import tpu as pltpu
from jax.sharding import Mesh, PartitionSpec as P

D = 768
H = 12
HD = 64
FF = 3072
BLK = 64
TP = 4
HL = H // TP
HW = HL * HD
COLS = 640
TOK = 128
ROWS = TOK * TP
KEYS = 4096
CHUNK = 2048
BACK = 2048
EPS = 1e-05
MASKED = -1e30
LOG2E = 1.4426950408889634
SCALE = HD**-0.5
BF = jnp.bfloat16
F32 = jnp.float32
G = ("c", "y", "z")
SWAP = ((0, 1), (1, 0))


def natural_feature(i):
    c, y, z, x, r = i // 384, (i // 96) % 4, (i // 24) % 4, (i // 6) % 4, i % 6
    return y * 192 + z * 48 + x * 12 + c * 6 + r


def feature_matrix():
    out = np.zeros((D, D), np.float32)
    i = np.arange(D)
    out[natural_feature(i), i] = 1
    return out.astype(jnp.bfloat16)


def head_matrix():
    out = np.zeros((COLS, 6 * 2 * HD), np.float32)
    for h in range(HL):
        for d in range(HD):
            out[HW + h * HD + d, h * 128 + d] = 1
            out[2 * HW + h * HD + d, h * 128 + HD + d] = 1
            out[h * HD + d, 384 + h * 128 + d] = 1
    return out.astype(jnp.bfloat16)


def place_matrix():
    out = np.zeros((2 * HW, 384), np.float32)
    for h in range(HL):
        for d in range(HD):
            out[HW + h * HD + d, h * 128 + HD + d] = 1
    return out.astype(jnp.bfloat16)


def dot(a, b):
    return lax.dot_general(a, b, (((1,), (0,)), ((), ())), preferred_element_type=F32)


def dot_nt(a, b):
    return lax.dot_general(a, b, (((1,), (1,)), ((), ())), preferred_element_type=F32)


def dot_tn(a, b):
    return lax.dot_general(a, b, (((0,), (0,)), ((), ())), preferred_element_type=F32)


def standardized(v):
    mean = jnp.mean(v, -1, keepdims=True)
    centered = v - mean
    rstd = lax.rsqrt(jnp.mean(centered * centered, -1, keepdims=True) + EPS)
    return centered * rstd, rstd


def norm_back(g, xhat, rstd):
    return rstd * (
        g - jnp.mean(g, -1, keepdims=True) - xhat * jnp.mean(g * xhat, -1, keepdims=True)
    )


def gelu_pair(u):
    k = 0.7978845608028654
    t = jnp.tanh(k * (u + 0.044715 * u * u * u))
    value = 0.5 * u * (1 + t)
    slope = 0.5 * (1 + t) + 0.5 * u * (1 - t * t) * k * (1 + 3 * 0.044715 * u * u)
    return value, slope


TILES = ((0, KEYS // 2), (ROWS // 2, KEYS))


def scores_t(kv, q, qpos, start, masked):
    s = dot_nt(kv, q)
    if masked:
        key = lax.broadcasted_iota(jnp.int32, s.shape, 0) + start
        s = jnp.where(key <= qpos, s, MASKED)
    return s


def attend_kernel(
    kpos, rank, qpos_ref, q_ref, own_ref, other_ref, o_ref, ot_ref, lse_ref, kvs_ref, kvt_ref, qs_ref, o_s, o_r
):
    head = pl.program_id(0)
    for b in range(KEYS // BLK):
        at = pl.multiple_of(kpos[b] * BLK, BLK)
        part = own_ref if b < KEYS // BLK // 2 else other_ref
        row = b % (KEYS // BLK // 2) * BLK
        kvs_ref[pl.ds(at, BLK), :] = part[row : row + BLK, :]
    for b in range(ROWS // BLK):
        at = pl.multiple_of(rank[b] * BLK, BLK)
        qs_ref[pl.ds(at, BLK), :] = q_ref[b * BLK : (b + 1) * BLK, :] * SCALE
    for i in range(KEYS // CHUNK):
        kvt_ref[:, i * CHUNK : (i + 1) * CHUNK] = kvs_ref[i * CHUNK : (i + 1) * CHUNK, :].T
    for first, span in TILES:
        q = qs_ref[first : first + 256, :]
        qpos = qpos_ref[0:1, first : first + 256]
        top = jnp.full((8, 256), MASKED, F32)
        for start in range(0, span, CHUNK):
            masked = start + CHUNK > span - KEYS // 2
            s = scores_t(kvs_ref[start : start + CHUNK, :], q, qpos, start, masked)
            top = jnp.maximum(top, jnp.max(s.reshape(-1, 8, 256), 0))
        top = jnp.max(top, 0, keepdims=True) * LOG2E
        mass = jnp.zeros((8, 256), F32)
        acc = jnp.zeros((128, 256), F32)
        for start in range(0, span, CHUNK):
            masked = start + CHUNK > span - KEYS // 2
            s = scores_t(kvs_ref[start : start + CHUNK, :], q, qpos, start, masked)
            p = jnp.exp2(s * LOG2E - top)
            mass = mass + jnp.sum(p.reshape(-1, 8, 256), 0)
            acc = acc + dot(kvt_ref[:, start : start + CHUNK], p.astype(BF))
        mass = jnp.sum(mass, 0, keepdims=True)
        o = acc[HD:, :] * (1.0 / mass)
        ot_ref[:, first : first + 256] = o
        o_s[pl.ds(pl.multiple_of(head * HD, HD), HD), first : first + 256] = o
        lse_ref[0, :, first : first + 256] = jnp.broadcast_to(top + jnp.log2(mass), (8, 256))

    @pl.when(head == HL - 1)
    def _():
        o_r[...] = o_s[...].T.astype(BF)
        for b in range(ROWS // BLK):
            at = pl.multiple_of(rank[b] * BLK, BLK)
            row, col = b * BLK % TOK, b * BLK // TOK * HW
            o_ref[row : row + BLK, col : col + HW] = o_r[pl.ds(at, BLK), :]


def attend_back_kernel(
    kpos,
    rank,
    qpos_ref,
    qs_ref,
    kvs_ref,
    kvt_ref,
    dbr_ref,
    place_ref,
    o_ref,
    lse_ref,
    own_ref,
    other_ref,
    dq_ref,
    dos,
    acc,
):
    do_all = dot(dbr_ref[...], place_ref[...]).astype(BF)
    for b in range(ROWS // BLK):
        at = pl.multiple_of(rank[b] * BLK, BLK)
        dos[pl.ds(at, BLK), :] = do_all[b * BLK : (b + 1) * BLK, :]
    dot_t = dos[...].astype(F32).T
    delta = jnp.sum(dot_t[HD:, :] * o_ref[...], 0, keepdims=True)
    dq = [jnp.zeros((128, 256), F32), jnp.zeros((128, 256), F32)]
    for start in range(0, KEYS, BACK):
        kv = kvs_ref[start : start + BACK, :]
        kvt = kvt_ref[:, start : start + BACK]
        total = None
        for n, (first, span) in enumerate(TILES):
            if start >= span:
                continue
            cols = slice(first, first + 256)
            q = qs_ref[cols, :]
            do = dos[cols, :]
            s = scores_t(kv, q, qpos_ref[0:1, cols], start, start + BACK > span - KEYS // 2)
            p = jnp.exp2(s * LOG2E - lse_ref[0, 0:1, cols])
            dp = dot_nt(kv, do)
            ds = (p * (dp - delta[:, cols])).astype(BF)
            part = dot(ds, q) + dot(p.astype(BF), do)
            total = part if total is None else total + part
            dq[n] = dq[n] + dot(kvt, ds)
        acc[start : start + BACK, :] = total.astype(BF)
    for b in range(KEYS // BLK):
        at = pl.multiple_of(kpos[b] * BLK, BLK)
        part = own_ref if b < KEYS // BLK // 2 else other_ref
        row = b % (KEYS // BLK // 2) * BLK
        part[row : row + BLK, :] = acc[pl.ds(at, BLK), :]
    dos[0:256, :] = (dq[0] * SCALE).T.astype(BF)
    dos[256:512, :] = (dq[1] * SCALE).T.astype(BF)
    for b in range(ROWS // BLK):
        at = pl.multiple_of(rank[b] * BLK, BLK)
        dq_ref[b * BLK : (b + 1) * BLK, :] = dos[pl.ds(at, BLK), :]


def settings(flops):
    return dict(
        compiler_params=pltpu.CompilerParams(vmem_limit_bytes=56 * 1024 * 1024),
        cost_estimate=pl.CostEstimate(flops=flops, bytes_accessed=8_000_000, transcendentals=0),
    )


def shape(dims, kind=BF):
    return jax.ShapeDtypeStruct(dims, kind)


def attend(kpos, rank, qpos, q, own, other):
    grid_spec = pltpu.PrefetchScalarGridSpec(
        num_scalar_prefetch=2,
        grid=(HL,),
        in_specs=[
            pl.BlockSpec((8, ROWS), lambda h, *_: (0, 0)),
            pl.BlockSpec((ROWS, 128), lambda h, *_: (0, h)),
            pl.BlockSpec((KEYS // 2, 128), lambda h, *_: (0, h)),
            pl.BlockSpec((KEYS // 2, 128), lambda h, *_: (0, h)),
        ],
        out_specs=[
            pl.BlockSpec((TOK, D), lambda h, *_: (0, 0)),
            pl.BlockSpec((HD, ROWS), lambda h, *_: (h, 0)),
            pl.BlockSpec((1, 8, ROWS), lambda h, *_: (h, 0, 0)),
            pl.BlockSpec((KEYS, 128), lambda h, *_: (0, h)),
            pl.BlockSpec((128, KEYS), lambda h, *_: (h, 0)),
            pl.BlockSpec((ROWS, 128), lambda h, *_: (0, h)),
        ],
        scratch_shapes=[pltpu.VMEM((HW, ROWS), F32), pltpu.VMEM((ROWS, HW), BF)],
    )
    return pl.pallas_call(
        attend_kernel,
        grid_spec=grid_spec,
        out_shape=[
            shape((TOK, D)),
            shape((HW, ROWS), F32),
            shape((HL, 8, ROWS), F32),
            shape((KEYS, 384)),
            shape((384, KEYS)),
            shape((ROWS, 384)),
        ],
        name="attend",
        **settings(5_000_000_000),
    )(kpos, rank, qpos, q, own, other)


def attend_back(kpos, rank, qpos, qs, kvs, kvt, dbr, place, o, lse):
    grid_spec = pltpu.PrefetchScalarGridSpec(
        num_scalar_prefetch=2,
        grid=(HL,),
        in_specs=[
            pl.BlockSpec((8, ROWS), lambda h, *_: (0, 0)),
            pl.BlockSpec((ROWS, 128), lambda h, *_: (0, h)),
            pl.BlockSpec((KEYS, 128), lambda h, *_: (0, h)),
            pl.BlockSpec((128, KEYS), lambda h, *_: (h, 0)),
            pl.BlockSpec((ROWS, 2 * HW), lambda h, *_: (0, 0)),
            pl.BlockSpec((2 * HW, 128), lambda h, *_: (0, h)),
            pl.BlockSpec((HD, ROWS), lambda h, *_: (h, 0)),
            pl.BlockSpec((1, 8, ROWS), lambda h, *_: (h, 0, 0)),
        ],
        out_specs=[
            pl.BlockSpec((KEYS // 2, 128), lambda h, *_: (0, h)),
            pl.BlockSpec((KEYS // 2, 128), lambda h, *_: (0, h)),
            pl.BlockSpec((ROWS, 128), lambda h, *_: (0, h)),
        ],
        scratch_shapes=[pltpu.VMEM((ROWS, 128), BF), pltpu.VMEM((KEYS, 128), BF)],
    )
    return pl.pallas_call(
        attend_back_kernel,
        grid_spec=grid_spec,
        out_shape=[shape((KEYS // 2, 384)), shape((KEYS // 2, 384)), shape((ROWS, 384))],
        name="attend_back",
        **settings(15_000_000_000),
    )(kpos, rank, qpos, qs, kvs, kvt, dbr, place, o, lse)


GAIN1, BIAS1, BQ, BV, BOUT, GAIN2, BIAS2, BFC2, BFC1 = range(9)


def project_kernel(
    c_ref, rows_ref, own_ref, other_ref, heads_ref, perm_t_ref, a1_ref, kv_ref, q_ref, vec_ref, w_ref
):
    c = c_ref[0]
    w_ref[pl.ds(pl.multiple_of(c * (D // 2), D // 2), D // 2), :] = own_ref[...]
    w_ref[pl.ds(pl.multiple_of((1 - c) * (D // 2), D // 2), D // 2), :] = other_ref[...]
    vec = w_ref[:, 512:].astype(F32).T[64:80]
    vec_ref[...] = vec
    bqv = dot_nt(vec[0:8].astype(BF), perm_t_ref[...]).astype(BF)
    bias = (
        dot(bqv, heads_ref[0:HW, :])[BQ : BQ + 1]
        + dot(bqv, heads_ref[2 * HW : 3 * HW, :])[BV : BV + 1]
    )
    w = dot(w_ref[...], heads_ref[...]).astype(BF)
    for i in range(TP):
        at = slice(i * TOK, (i + 1) * TOK)
        hat, _ = standardized(rows_ref[i, 0:TOK, :].astype(F32))
        a1_ref[at, :] = (hat * vec[GAIN1 : GAIN1 + 1] + vec[BIAS1 : BIAS1 + 1]).astype(BF)
    for i in range(2):
        at = slice(i * 256, (i + 1) * 256)
        qkv = (dot(a1_ref[at, :], w) + bias).astype(BF)
        q_ref[at, :] = qkv[:, 384:]
        for j in range(4):
            kv_ref[j, at, :] = qkv[:, :384]


def project(c, rows, own, other, heads, perm_t):
    half = pl.BlockSpec((D // 2, COLS), lambda i: (0, 0))
    return pl.pallas_call(
        project_kernel,
        grid=(1,),
        in_specs=[
            pl.BlockSpec(memory_space=pltpu.SMEM),
            pl.BlockSpec((TP, TOK, D), lambda i: (0, 0, 0)),
            half,
            half,
            pl.BlockSpec((COLS, D), lambda i: (0, 0)),
            pl.BlockSpec((HW, D), lambda i: (0, 0)),
        ],
        out_specs=[
            pl.BlockSpec((ROWS, D), lambda i: (0, 0)),
            pl.BlockSpec((4, ROWS, 384), lambda i: (0, 0, 0)),
            pl.BlockSpec((ROWS, 384), lambda i: (0, 0)),
            pl.BlockSpec((16, D), lambda i: (0, 0)),
            pl.BlockSpec((D, COLS), lambda i: (0, 0)),
        ],
        out_shape=[
            shape((ROWS, D)),
            shape((4, ROWS, 384)),
            shape((ROWS, 384)),
            shape((16, D), F32),
            shape((D, COLS)),
        ],
        name="project",
        **settings(2_000_000_000),
    )(c, rows, own, other, heads, perm_t)


def feed_kernel(
    x_ref,
    o_ref,
    rows_ref,
    perm_ref,
    w_ref,
    vec_ref,
    da2_ref,
    act_ref,
    a2_ref,
    du_ref,
    resid_ref,
    op_ref,
    resid_s,
    w_s,
    sems,
):
    copies = [
        pltpu.make_async_copy(w_ref.at[:, pl.ds(i * D, D)], w_s.at[i], sems.at[i]) for i in range(3)
    ]
    for i in (1, 0, 2):
        copies[i].start()
    vec = vec_ref[...]
    for i in range(2):
        at = slice(i * 256, (i + 1) * 256)
        op = None
        for j in range(TP):
            first = o_ref[j, :, 2 * i * HW : (2 * i + 1) * HW]
            later = o_ref[j, :, (2 * i + 1) * HW : (2 * i + 2) * HW]
            part = dot(jnp.concatenate([first, later], 0), perm_ref[j * HW : (j + 1) * HW, :])
            op = part if op is None else op + part
        op = op.astype(BF)
        op_ref[at, :] = op
        tok = jnp.concatenate([rows_ref[2 * i, 0:TOK, :], rows_ref[2 * i + 1, 0:TOK, :]], 0)
        dy = jnp.concatenate([rows_ref[2 * i, TOK:, :], rows_ref[2 * i + 1, TOK:, :]], 0)
        if i == 0:
            copies[1].wait()
        resid = tok.astype(F32) + dot(op, w_s[1]) + vec[BOUT : BOUT + 1]
        resid_s[at, :] = resid
        hat, _ = standardized(resid)
        a2 = (hat * vec[GAIN2 : GAIN2 + 1] + vec[BIAS2 : BIAS2 + 1]).astype(BF)
        a2_ref[at, :] = a2
        if i == 0:
            copies[0].wait()
        act, slope = gelu_pair(dot(a2, w_s[0]) + vec[BFC1 : BFC1 + 1])
        if i == 0:
            copies[2].wait()
        du = (dot_nt(dy, w_s[2]) * slope).astype(BF)
        du_ref[at, :] = du
        act_ref[at, :] = act.astype(BF)
        da2 = dot_nt(du, w_s[0]).astype(BF)
        da2_ref[2 * i] = da2[:TOK]
        da2_ref[2 * i + 1] = da2[TOK:]
    resid_ref[...] = resid_s[pl.ds(pl.multiple_of(x_ref[0] * TOK, TOK), TOK), :]


def feed(x, o, rows, perm, w, vec):
    whole = pl.BlockSpec(memory_space=pltpu.VMEM)
    return pl.pallas_call(
        feed_kernel,
        in_specs=[pl.BlockSpec(memory_space=pltpu.SMEM)]
        + [whole] * 3
        + [pl.BlockSpec(memory_space=pl.ANY), whole],
        out_specs=[whole] * 6,
        out_shape=[
            shape((TP, TOK, D)),
            shape((ROWS, D)),
            shape((ROWS, D)),
            shape((ROWS, D)),
            shape((TOK, D), F32),
            shape((ROWS, D)),
        ],
        scratch_shapes=[
            pltpu.VMEM((ROWS, D), F32),
            pltpu.VMEM((3, D, D), BF),
            pltpu.SemaphoreType.DMA((3,)),
        ],
        name="feed",
        **settings(4_000_000_000),
    )(x, o, rows, perm, w, vec)


def feed_grads_kernel(
    rows_ref,
    perm_ref,
    w2_ref,
    act_ref,
    a2_ref,
    du_ref,
    gw_ref,
    mixed_ref,
    gb_ref,
    dy_s,
    g_s,
):
    for i in range(TP):
        at = slice(i * TOK, (i + 1) * TOK)
        dy_s[at, :] = dot_nt(rows_ref[i, TOK:, :], perm_ref[...]).astype(BF)
    for lhs, rhs, col in ((a2_ref, du_ref, 0), (act_ref, dy_s, D)):
        for core in range(2):
            part = dot_tn(lhs[:, core * 384 : (core + 1) * 384], rhs[...])
            for y in range(4):
                for z in range(4):
                    to = ((core * 4 + z) * 4 + y) * 24
                    g_s[to : to + 24, :] = part[(y * 4 + z) * 24 : (y * 4 + z + 1) * 24]
        gw_ref[:, col : col + D] = g_s[...].astype(BF)
    for i in range(2):
        at = slice(i * 256, (i + 1) * 256)
        mixed_ref[at, :] = dot(act_ref[at, :], w2_ref[...]).astype(BF)
    gb_ref[...] = jnp.broadcast_to(jnp.sum(du_ref[...].astype(F32), 0, keepdims=True), (8, D))


def feed_grads(rows, perm, w, act, a2, du):
    whole = pl.BlockSpec((ROWS, D), lambda i: (0, 0))
    return pl.pallas_call(
        feed_grads_kernel,
        grid=(1,),
        in_specs=[
            pl.BlockSpec((TP, 2 * TOK, D), lambda i: (0, 0, 0)),
            pl.BlockSpec((D, D), lambda i: (0, 0)),
            pl.BlockSpec((D, D), lambda i: (0, 2)),
            whole,
            whole,
            whole,
        ],
        out_specs=[
            pl.BlockSpec((D, 2 * D), lambda i: (0, 0)),
            whole,
            pl.BlockSpec((8, D), lambda i: (0, 0)),
        ],
        out_shape=[shape((D, 2 * D)), shape((ROWS, D)), shape((8, D), F32)],
        scratch_shapes=[pltpu.VMEM((ROWS, D), BF), pltpu.VMEM((D, D), F32)],
        name="feed_grads",
        **settings(3_000_000_000),
    )(rows, perm, w, act, a2, du)


def norm2_kernel(
    da2_ref, resid_ref, dy_ref, vec_ref, wo_ref, perm_ref, send_ref, dresid_ref, sums_ref
):
    da2 = da2_ref[0].astype(F32)
    for i in range(1, TP):
        da2 = da2 + da2_ref[i].astype(F32)
    hat, rstd = standardized(resid_ref[...])
    dy = dy_ref[...].astype(F32)
    dresid = dy + norm_back(da2 * vec_ref[GAIN2 : GAIN2 + 1, :], hat, rstd)
    dresid_ref[...] = dresid
    dbr = dresid.astype(BF)
    do = dot_nt(dbr, wo_ref[...]).astype(BF)
    dbr_nat = dot_nt(dbr, perm_ref[...]).astype(BF)
    do_nat = dot_nt(do, perm_ref[...]).astype(BF)
    for i in range(TP):
        send_ref[i, :, 0:HW] = dbr_nat[:, i * HW : (i + 1) * HW]
        send_ref[i, :, HW:] = do_nat[:, i * HW : (i + 1) * HW]
    sums_ref[0:1, :] = jnp.sum(dbr.astype(F32), 0, keepdims=True)
    sums_ref[1:2, :] = jnp.sum(da2 * hat, 0, keepdims=True)
    sums_ref[2:3, :] = jnp.sum(da2, 0, keepdims=True)
    sums_ref[3:4, :] = jnp.sum(dy, 0, keepdims=True)
    sums_ref[4:8, :] = jnp.zeros((4, D), F32)


def norm2(da2, resid, dy, vec, w, perm):
    def whole(*dims):
        return pl.BlockSpec(dims, lambda i: (0,) * len(dims))

    return pl.pallas_call(
        norm2_kernel,
        grid=(1,),
        in_specs=[
            whole(TP, TOK, D),
            whole(TOK, D),
            pl.BlockSpec((TOK, D), lambda i: (1, 0)),
            whole(16, D),
            pl.BlockSpec((D, D), lambda i: (0, 1)),
            whole(D, D),
        ],
        out_specs=[whole(TP, TOK, 2 * HW), whole(TOK, D), whole(8, D)],
        out_shape=[shape((TP, TOK, 2 * HW)), shape((TOK, D), F32), shape((8, D), F32)],
        name="norm2",
        **settings(100_000_000),
    )(da2, resid, dy, vec, w, perm)


def early_kernel(dq_ref, heads_ref, a1_ref, op_ref, dbr_ref, dqn_ref, pack_ref):
    dq = dot_nt(dq_ref[...], heads_ref[0:256, 384:]).astype(BF)
    dqn_ref[...] = dq
    dbr_t = dbr_ref[:, 0:HW]
    for i in range(3):
        at = slice(i * 256, (i + 1) * 256)
        pack_ref[at, 0:256] = dot_tn(a1_ref[:, at], dq).astype(BF)
        pack_ref[at, 256 : 256 + HW] = dot_tn(op_ref[:, at], dbr_t).astype(BF)
        pack_ref[at, 256 + HW :] = jnp.zeros((256, 64), BF)


def early(dq, heads, a1, op, dbr):
    return pl.pallas_call(
        early_kernel,
        out_shape=[shape((ROWS, 256)), shape((D, 512))],
        name="early",
        **settings(1_000_000_000),
    )(dq, heads, a1, op, dbr)


def grads_kernel(
    c_ref,
    dkv_ref,
    dqn_ref,
    early_ref,
    heads_ref,
    w_ref,
    a1_ref,
    rows_ref,
    perm_t_ref,
    gb_ref,
    sums_ref,
    da1_ref,
    own_ref,
    other_ref,
    g_s,
    dqkv_s,
    pack_ref,
):
    ones = jnp.zeros((1, D), F32)
    gain, bias = ones, ones
    for i in range(2):
        at = slice(i * 256, (i + 1) * 256)
        dkv = dkv_ref[0, at, :].astype(F32)
        for j in range(1, 4):
            dkv = dkv + dkv_ref[j, at, :].astype(F32)
        dqkv = dot_nt(dkv.astype(BF), heads_ref[:, :384]).astype(BF)
        dqkv_s[at, :] = dqkv
        dqkv_s[at, 0:128] = dqn_ref[at, 0:128]
        dqkv_s[at, 128:256] = dqkv[:, 128:256] + dqn_ref[at, 128:256]
        da1 = dot_nt(dqkv_s[at, :], w_ref[...])
        da1_ref[at, :] = da1.astype(BF)
        tok = jnp.concatenate([rows_ref[2 * i], rows_ref[2 * i + 1]], 0)
        hat, _ = standardized(tok.astype(F32))
        gain = gain + jnp.sum(da1 * hat, 0, keepdims=True)
        bias = bias + jnp.sum(da1, 0, keepdims=True)
    dsum = jnp.sum(dqkv_s[...].astype(F32), 0, keepdims=True).astype(BF)
    dsum = jnp.broadcast_to(dsum, (8, COLS))
    lanes = lax.broadcasted_iota(jnp.int32, (COLS, HW), 0)
    head = lax.broadcasted_iota(jnp.int32, (COLS, HW), 1)
    g_bq = dot(dot(dsum, (lanes == head).astype(BF)).astype(BF), perm_t_ref[...])
    g_bv = dot(dot(dsum, (lanes == head + 2 * HW).astype(BF)).astype(BF), perm_t_ref[...])
    g_s[...] = jnp.zeros((128, D), F32)
    g_s[64 + GAIN1 : 65 + GAIN1, :] = gain
    g_s[64 + BIAS1 : 65 + BIAS1, :] = bias
    g_s[64 + BQ : 65 + BQ, :] = g_bq[0:1]
    g_s[64 + BV : 65 + BV, :] = g_bv[0:1]
    g_s[64 + BOUT : 64 + BOUT + 4, :] = sums_ref[0:4, :]
    g_s[64 + BFC1 : 65 + BFC1, :] = gb_ref[0:1, :]
    pack_ref[:, 0:128] = early_ref[:, 0:128]
    pack_ref[:, COLS:] = early_ref[:, 256:]
    for i in range(3):
        at = slice(i * 256, (i + 1) * 256)
        g = dot_tn(a1_ref[:, at], dqkv_s[:, 128:])
        pack_ref[at, 128:512] = g[:, :384].astype(BF)
        pack_ref[at, 512:COLS] = (g[:, 384:] + g_s[:, at].T).astype(BF)
    c = c_ref[0]
    own_ref[...] = pack_ref[pl.ds(pl.multiple_of(c * (D // 2), D // 2), D // 2), :]
    other_ref[...] = pack_ref[pl.ds(pl.multiple_of((1 - c) * (D // 2), D // 2), D // 2), :]


def grads(c, dkv, dqn, pack, heads, w, a1, rows, perm_t, gb, sums):
    def whole(*dims):
        return pl.BlockSpec(dims, lambda i: (0,) * len(dims))

    return pl.pallas_call(
        grads_kernel,
        grid=(1,),
        in_specs=[
            pl.BlockSpec(memory_space=pltpu.SMEM),
            whole(4, ROWS, 384),
            whole(ROWS, 256),
            whole(D, 512),
            whole(COLS, 384),
            whole(D, COLS),
            whole(ROWS, D),
            whole(TP, TOK, D),
            whole(HW, D),
            whole(8, D),
            whole(8, D),
        ],
        out_specs=[whole(ROWS, D), whole(D // 2, 896), whole(D // 2, 896)],
        out_shape=[shape((ROWS, D)), shape((D // 2, 896)), shape((D // 2, 896))],
        scratch_shapes=[
            pltpu.VMEM((128, D), F32),
            pltpu.VMEM((ROWS, COLS), BF),
            pltpu.VMEM((D, 896), BF),
        ],
        name="grads",
        **settings(2_000_000_000),
    )(c, dkv, dqn, pack, heads, w, a1, rows, perm_t, gb, sums)


def exchange(v, axes):
    return lax.all_to_all(v, axes, 0, 0, tiled=True)


def spread(v, axes, n):
    return exchange(jnp.broadcast_to(v[None], (n,) + v.shape), axes)


def per_device(
    tokens,
    cotangent,
    block_map,
    ln1_gain,
    ln1_bias,
    w_qkv,
    b_query,
    b_value,
    w_out,
    b_out,
    ln2_gain,
    ln2_bias,
    w_fc1,
    b_fc1,
    w_fc2,
    b_fc2,
):
    perm = jnp.asarray(feature_matrix())
    heads = jnp.asarray(head_matrix())
    z, x, c = lax.axis_index("z"), lax.axis_index("x"), lax.axis_index("c")
    perm_t = lax.dynamic_slice_in_dim(perm, x * HW, HW, 0)

    maps = block_map.reshape(4, 4, 2, 2).transpose(2, 0, 1, 3)
    maps = jnp.where(c == 0, maps, maps[::-1])
    kpos = maps.reshape(-1)
    own = lax.dynamic_slice(maps[0], (z, 0, 0), (1, 4, 2)).reshape(-1)
    before = own[None, :] < own[:, None]
    rank = jnp.sum(before.astype(jnp.int32), 1)
    ordered = jnp.sum(jnp.where(rank[:, None] == jnp.arange(8)[None, :], own[:, None], 0), 0)
    qpos = (ordered[:, None] * BLK + jnp.arange(BLK, dtype=jnp.int32)[None, :]).reshape(1, -1)
    qpos = jnp.broadcast_to(qpos, (8, ROWS))

    out_cols = dot(jnp.concatenate([w_out, w_fc2], 0), perm).astype(BF)
    vectors = (ln1_gain, ln1_bias, b_query, b_value, b_out, ln2_gain, ln2_bias, b_fc2)
    vectors = sum(jnp.pad(v, (6 * i, 42 - 6 * i)) for i, v in enumerate(vectors))
    vectors = jnp.pad(vectors.reshape(8, 6).T, ((0, 0), (0, 56)))
    qkv_cols = w_qkv.reshape(6, 3, TP, HW).transpose(2, 0, 1, 3).reshape(TP, 6, 3 * HW)
    fc1_cols = w_fc1.reshape(6, 16, TP, 2, 24).transpose(2, 0, 3, 1, 4).reshape(TP, 6, D)
    sent = jnp.concatenate(
        [
            qkv_cols,
            jnp.broadcast_to(vectors[None], (TP, 6, 64)),
            fc1_cols,
            jnp.broadcast_to(out_cols[None, :6], (TP, 6, D)),
        ],
        2,
    )
    both = jnp.concatenate([tokens[0], cotangent[0]], 0)
    own_rows = dot(both, perm).astype(BF)
    all_rows = lax.all_gather(own_rows, "x", axis=0)

    got = exchange(sent, "x").reshape(24, -1)
    got, perm_t = lax.optimization_barrier((got, perm_t))
    first = jnp.where(
        jnp.arange(COLS)[None, :] == 3 * HW + BFC1, b_fc1[:, None], got[:, :COLS]
    )
    first = spread(first, ("y", "z"), 16).reshape(D // 2, COLS)
    other = lax.ppermute(first, "c", SWAP)
    rest = jnp.concatenate([got[:, COLS:], out_cols[6:]], 1)
    other, rest = lax.optimization_barrier((other, rest))
    second = lax.all_gather(rest, G, axis=0, tiled=True)

    core = c.reshape(1)
    a1, kv, q, vec, w_heads = project(core, all_rows, first, other, heads, perm_t)
    kv = exchange(kv, "z").reshape(KEYS // 2, 384)
    other = lax.ppermute(kv, "c", SWAP)
    o, o_t, lse, kvs, kvt, qs = attend(kpos, rank, qpos, q, kv, other)
    o = lax.all_gather(o, "x", axis=0)
    da2_part, act, a2, du, resid, o_perm = feed(x.reshape(1), o, all_rows, perm, second, vec)
    g_feed, mixed_part, g_bfc1 = feed_grads(all_rows, perm, second, act, a2, du)

    da2 = exchange(da2_part, "x")
    da2, g_feed = lax.optimization_barrier((da2, g_feed))
    dbr, dresid, sums = norm2(da2, resid, own_rows, vec, second, perm)
    r_feed = lax.psum_scatter(g_feed, ("c", "z"), scatter_dimension=0, tiled=True)
    dbr = exchange(dbr, "x").reshape(ROWS, 2 * HW)
    dbr, mixed_part = lax.optimization_barrier((dbr, mixed_part))
    mixed_part = exchange(mixed_part.reshape(TP, TOK, D), "x")
    dkv, dkv_other, dq = attend_back(
        kpos, rank, qpos, qs, kvs, kvt, dbr, jnp.asarray(place_matrix()), o_t, lse
    )
    dkv_other, mixed_part, r_feed = lax.optimization_barrier((dkv_other, mixed_part, r_feed))
    r_feed = lax.psum_scatter(r_feed, "y", scatter_dimension=0, tiled=True)
    dkv_other = lax.ppermute(dkv_other, "c", SWAP)
    mixed = jnp.sum(mixed_part.astype(F32), 0)
    mixed = (resid + mixed + vec[BFC2 : BFC2 + 1]).astype(BF)
    mixed = dot_nt(mixed, perm).astype(BF)
    dkv = (dkv.astype(F32) + dkv_other.astype(F32)).astype(BF).reshape(4, ROWS, 384)
    dkv = exchange(dkv, "z")
    dkv, r_feed = lax.optimization_barrier((dkv, r_feed))
    dqn, pack = early(dq, heads, a1, o_perm, dbr)
    da1_part, pack, pack_other = grads(
        core, dkv, dqn, pack, heads, w_heads, a1, all_rows, perm_t, g_bfc1, sums
    )
    da1 = lax.psum_scatter(da1_part, "x", scatter_dimension=0, tiled=True)
    da1 = da1.astype(F32)
    hat1, rstd1 = standardized(own_rows[:TOK].astype(F32))
    dtok = (dresid + norm_back(da1 * vec[GAIN1 : GAIN1 + 1], hat1, rstd1)).astype(BF)
    dtok = dot_nt(dtok, perm).astype(BF)

    r_feed = r_feed.astype(F32)
    pack_other = lax.ppermute(pack_other, "c", SWAP)
    half = (pack.astype(F32) + pack_other.astype(F32)).astype(BF)
    mine = jnp.sum(exchange(half, ("y", "z")).reshape(16, 24, -1).astype(F32), 0)
    r_fc1 = r_feed[:, :D].reshape(24, 2, 16, 24).transpose(0, 2, 1, 3).reshape(24, D)
    last = jnp.concatenate([mine[:, : COLS + HW], r_fc1], 1).astype(BF)
    last = exchange(last.reshape(TP, 6, -1), "x")
    last, dtok, mixed = lax.optimization_barrier((last, dtok, mixed))
    last = last.astype(F32)
    r_qkv = last[:, :, : 3 * HW].reshape(TP, 6, 3, HW).transpose(1, 2, 0, 3).reshape(6, 3 * D)
    r_out = last[:, :, COLS : COLS + HW].transpose(1, 0, 2).reshape(6, D)
    r_fc1 = last[:, :, COLS + HW :].reshape(TP, 6, 16, 48).transpose(1, 2, 0, 3).reshape(6, FF)
    r_vec = jnp.sum(last[:, :, 3 * HW : 3 * HW + 8], 0)
    return (
        mixed[None],
        dtok[None],
        r_vec[:, GAIN1],
        r_vec[:, BIAS1],
        r_qkv,
        r_vec[:, BQ],
        r_vec[:, BV],
        r_out,
        r_vec[:, BOUT],
        r_vec[:, GAIN2],
        r_vec[:, BIAS2],
        r_fc1,
        mine[:, 3 * HW + BFC1],
        r_feed[:, D:],
        r_vec[:, BFC2],
    )


def solution(mesh):
    fine = Mesh(mesh.devices.reshape(4, 4, 4, 2), ("y", "z", "x", "c"))
    rows = P("y", ("z", "x", "c"), None)
    every = ("y", "z", "x", "c")
    vec, mat = P(every), P(every, None)
    in_specs = (rows, rows, P(), vec, vec, mat, vec, vec, mat, vec, vec, vec, mat, vec, mat, vec)
    out_specs = (rows, rows, vec, vec, mat, vec, vec, mat, vec, vec, vec, mat, vec, mat, vec)
    return jax.shard_map(
        per_device, mesh=fine, in_specs=in_specs, out_specs=out_specs, check_vma=False
    )
```
